32 devices in a mesh: ctx: 16 (over z, y, x), tp: 2 (over core).
Axes of the slice: x: 2, y: 2, z: 4, core: 2. Of those that a mesh axis runs over, the one named last changes fastest.
Arguments:
- queries: bfloat16 [4096, 4096], P('ctx', 'tp'), may hold values from -6 to 6
- keys: bfloat16 [4096, 4096], P('ctx', 'tp'), may hold values from -6 to 6
- values: bfloat16 [4096, 4096], P('ctx', 'tp'), may hold values from -6 to 6
- gain: float32 [4096], P('tp'), may hold values from 0.5 to 1.5
- out_weight: bfloat16 [4096, 6144], P('ctx', 'tp'), may hold values from -0.125 to 0.125
- cotangent: bfloat16 [4096, 6144], P('ctx', 'tp'), may hold values from -6 to 6
Outputs:
- mixed: bfloat16 [4096, 6144], P('ctx', 'tp')
- grad_queries: bfloat16 [4096, 4096], P('ctx', 'tp')
- grad_keys: bfloat16 [4096, 4096], P('ctx', 'tp')
- grad_values: bfloat16 [4096, 4096], P('ctx', 'tp')
The draws below stay inside these ranges and needn't reach their ends.
All inputs are finite; a program needn't handle non-finite values.
Results may differ from the reference program's by a relative error of at most 0.005.
Values may be sent and summed in bfloat16 or wider, within the bound.
No kernel may reach another device: no remote copies, remote signals or barrier semaphores. Data moves between devices by JAX's collectives and lax.ppermute only.
A program may use at most 192 MiB of HBM per device.

```python
import jax
import jax.numpy as jnp
from jax import lax

D = 6144
H = 32
DH = 128
TOK_DEV = 256
SEQ = 4096


def strengthened(drawn, stream_key, source, target, blocks, factor):
    def block_of(position):
        return (jnp.arange(drawn.shape[position]) // (drawn.shape[position] // blocks)).reshape((-1,) + (1,) * (drawn.ndim - 1 - position))

    first = jax.random.permutation(stream_key, blocks)[block_of(target)]
    far = (block_of(target) + blocks // 2) % blocks
    return jnp.where((block_of(source) == first) | (block_of(source) == far), factor * drawn, drawn)


def level_of(stream_key, extent, shards, smallest, high):
    level, own = 1.0, jax.random.fold_in(stream_key, 6)
    for position, shards_of in shards:
        steps = jnp.exp(jax.random.uniform(jax.random.fold_in(own, position), (shards_of,), jnp.float32, smallest / len(shards), high / len(shards)))
        level = level * jnp.repeat(steps, extent[position] // shards_of).reshape([-1 if axis == position else 1 for axis in range(len(extent))])
    return level


def bell_draw(own_key, dims, scale, reach, shards=(), kind=jnp.bfloat16):
    values = jax.random.normal(own_key, dims, jnp.float32) * scale
    if len(shards) > 0:
        values = level_of(own_key, dims, shards, -0.22, 0.18) * values
    return jnp.clip(values, min=-reach, max=reach).astype(kind)


def bell_draw_with(rng, dims, scale, most, pieces, heavy, dtype=jnp.bfloat16):
    drawn = scale * jax.random.normal(rng, dims, jnp.float32)
    if pieces:
        drawn = drawn * level_of(rng, dims, pieces, -0.22, 0.18)
    return jnp.clip(strengthened(drawn, jax.random.fold_in(rng, 3), *heavy), -most, most).astype(dtype)


def setup_inputs(seed: int = 0) -> dict:
    key_list = jax.random.split(jax.random.key(seed), 7)
    return {
        "queries": bell_draw(key_list[0], (SEQ, H * DH), 1.0, 6.0, ((0, 16), (1, 2))),
        "keys": bell_draw(key_list[1], (SEQ, H * DH), 1.0, 6.0, ((0, 16), (1, 2))),
        "values": bell_draw(key_list[2], (SEQ, H * DH), 1.0, 6.0, ((0, 16), (1, 2))),
        "gain": jnp.clip(0.5 + 1.0 * jax.random.uniform(key_list[3], (H * DH,), jnp.float32) ** level_of(key_list[3], (H * DH,), ((0, 2),), -0.2, 0.2), 0.5, 1.5),
        "out_weight": bell_draw_with(key_list[4], (H * DH, D), (H * DH) ** -0.5, 0.125, ((0, 16), (1, 2)), (1, 0, 16, 2.0)),
        "cotangent": bell_draw(key_list[5], (SEQ, D), 1.0, 6.0, ((0, 16), (1, 2))),
    }


def reference(queries, keys, values, gain, out_weight, cotangent):
    blocks = SEQ // TOK_DEV
    highest = lax.Precision.HIGHEST

    def split(arr):
        return arr.astype(jnp.float32).reshape(blocks, TOK_DEV, H, DH)
    q_blocks = split(queries)
    k_blocks = split(keys)
    v_blocks = split(values)
    mask = jnp.tril(jnp.ones((TOK_DEV, TOK_DEV), jnp.float32))
    zero_state = jnp.zeros((H, DH, DH), jnp.float32)

    def forward(state, block):
        q_now, k_now, v_now = block
        scores = jnp.einsum('thd,shd->hts', q_now, k_now, precision=highest) * mask[None]
        out = jnp.einsum('hts,shd->thd', scores, v_now, precision=highest)
        out = out + jnp.einsum('thd,hde->the', q_now, state, precision=highest)
        new_state = state + jnp.einsum('thd,the->hde', k_now, v_now, precision=highest)
        return (new_state, (out, state))
    unused, (attn, earlier) = lax.scan(forward, zero_state, (q_blocks, k_blocks, v_blocks))
    attn = attn.reshape(SEQ, H, DH)
    gain_heads = gain.reshape(H, DH)
    rnorm = lax.rsqrt(lax.optimization_barrier(jnp.mean(attn * attn, axis=-1, keepdims=True)) + 1e-06)
    normed = attn * rnorm
    heads_out = (normed * gain_heads[None]).astype(jnp.bfloat16).reshape(SEQ, H * DH)
    mixed = jnp.dot(heads_out, out_weight, preferred_element_type=jnp.float32).astype(jnp.bfloat16)
    grad_heads = lax.dot_general(cotangent, out_weight, (((1,), (1,)), ((), ())), preferred_element_type=jnp.float32).reshape(SEQ, H, DH)
    scaled = grad_heads * gain_heads[None]
    grad_attn = rnorm * (scaled - normed * lax.optimization_barrier(jnp.mean(scaled * normed, axis=-1, keepdims=True)))
    g_blocks = grad_attn.reshape(blocks, TOK_DEV, H, DH)

    def backward(later, block):
        q_now, k_now, v_now, g_now, state = block
        scores = jnp.einsum('thd,shd->hts', q_now, k_now, precision=highest) * mask[None]
        weights = jnp.einsum('the,she->hts', g_now, v_now, precision=highest) * mask[None]
        grad_q = jnp.einsum('the,hde->thd', g_now, state, precision=highest)
        grad_q = grad_q + jnp.einsum('hts,shd->thd', weights, k_now, precision=highest)
        grad_k = jnp.einsum('she,hde->shd', v_now, later, precision=highest)
        grad_k = grad_k + jnp.einsum('hts,thd->shd', weights, q_now, precision=highest)
        grad_v = jnp.einsum('shd,hde->she', k_now, later, precision=highest)
        grad_v = grad_v + jnp.einsum('hts,the->she', scores, g_now, precision=highest)
        new_later = later + jnp.einsum('thd,the->hde', q_now, g_now, precision=highest)
        return (new_later, (grad_q, grad_k, grad_v))
    unused_two, (grad_q, grad_k, grad_v) = lax.scan(backward, zero_state, (q_blocks, k_blocks, v_blocks, g_blocks, earlier), reverse=True)

    def finish(arr):
        return arr.reshape(SEQ, H * DH).astype(jnp.bfloat16)
    return (mixed, finish(grad_q), finish(grad_k), finish(grad_v))
```

```python
import math

import jax
import jax.numpy as jnp
from jax import lax
from jax.experimental import pallas as pl
from jax.experimental.pallas import tpu as pltpu
from jax.sharding import PartitionSpec as P

DH = 128
F32 = jnp.float32
BF16 = jnp.bfloat16
PLANE = 4
PLANES = 4
CHUNKS = ((0, 1), (2, 3))
QUAD = 4
PAIR = 2
MIB = 1024 * 1024
LIGHT = pl.CostEstimate(flops=1, bytes_accessed=1, transcendentals=0)
NT = (((1,), (1,)), ((), ()))
TN = (((0,), (0,)), ((), ()))
NN = (((1,), (0,)), ((), ()))


def entering(value, axis, join, neutral, backward):
    count, mine = (lax.axis_size(axis), lax.axis_index(axis))
    pieces = lax.all_gather(value, axis)
    if backward:
        pieces = pieces[::-1]
        mine = count - 1 - mine
    running = jnp.full_like(value, 0) + jnp.asarray(neutral, value.dtype)

    def lap(position, running):
        longer = join(running, pieces[position])
        return jnp.where(position < mine, longer, running)

    return lax.fori_loop(0, count - 1, lap, running)


def add_states(earlier, later):
    return earlier + later


def local(queries, keys, values, gain, out_weight, cotangent):
    highest = lax.Precision.HIGHEST
    rows = queries.shape[0]
    heads = queries.shape[1] // DH
    q_heads = queries.reshape(rows, heads, DH)
    k_heads = keys.reshape(rows, heads, DH)
    v_heads = values.reshape(rows, heads, DH)
    q_float = q_heads.astype(jnp.float32)
    k_float = k_heads.astype(jnp.float32)
    v_float = v_heads.astype(jnp.float32)
    row_ids = lax.broadcasted_iota(jnp.int32, (rows, rows), 0)
    col_ids = lax.broadcasted_iota(jnp.int32, (rows, rows), 1)
    mask = (row_ids >= col_ids).astype(jnp.float32)
    zero_state = jnp.zeros((heads, DH, DH), jnp.float32)
    own_state = jnp.einsum("thd,the->hde", k_heads, v_heads, preferred_element_type=jnp.float32)
    prefix = entering(own_state, "ctx", add_states, zero_state, False)
    scores = (
        jnp.einsum("thd,shd->hts", q_heads, k_heads, preferred_element_type=jnp.float32)
        * mask[None]
    )
    attn = jnp.einsum("hts,shd->thd", scores, v_float, precision=highest)
    attn = attn + jnp.einsum("thd,hde->the", q_float, prefix, precision=highest)
    gain_heads = gain.reshape(heads, DH)
    rnorm = lax.rsqrt(jnp.mean(attn * attn, axis=-1, keepdims=True) + 1e-06)
    normed = attn * rnorm
    heads_out = (normed * gain_heads[None]).astype(jnp.bfloat16).reshape(rows, heads * DH)
    weight_all = lax.all_gather(out_weight, "ctx", axis=0, tiled=True)
    mixed = jnp.dot(
        lax.all_gather(heads_out, "tp", axis=1, tiled=True),
        weight_all,
        preferred_element_type=jnp.float32,
    ).astype(jnp.bfloat16)
    partial_grads = lax.dot_general(
        cotangent, weight_all, (((1,), (1,)), ((), ())), preferred_element_type=jnp.float32
    )
    grad_heads = lax.psum_scatter(partial_grads, "tp", scatter_dimension=1, tiled=True).reshape(
        rows, heads, DH
    )
    scaled = grad_heads * gain_heads[None]
    grad_attn = rnorm * (scaled - normed * jnp.mean(scaled * normed, axis=-1, keepdims=True))
    own_grad = jnp.einsum("thd,the->hde", q_float, grad_attn, precision=highest)
    later = entering(own_grad, "ctx", add_states, zero_state, True)
    weights = jnp.einsum("the,she->hts", grad_attn, v_float, precision=highest) * mask[None]
    grad_q = jnp.einsum("the,hde->thd", grad_attn, prefix, precision=highest)
    grad_q = grad_q + jnp.einsum("hts,shd->thd", weights, k_float, precision=highest)
    grad_k = jnp.einsum("she,hde->shd", v_float, later, precision=highest)
    grad_k = grad_k + jnp.einsum("hts,thd->shd", weights, q_float, precision=highest)
    grad_v = jnp.einsum("shd,hde->she", k_float, later, precision=highest)
    grad_v = grad_v + jnp.einsum("hts,the->she", scores, grad_attn, precision=highest)
    grad_queries = grad_q.reshape(rows, heads * DH).astype(jnp.bfloat16)
    grad_keys = grad_k.reshape(rows, heads * DH).astype(jnp.bfloat16)
    grad_values = grad_v.reshape(rows, heads * DH).astype(jnp.bfloat16)
    return (mixed, grad_queries, grad_keys, grad_values)


def mm(a, b, dims):
    return lax.dot_general(a, b, dims, preferred_element_type=F32)


def two_terms(value):
    high = value.astype(BF16)
    return high, (value - high.astype(F32)).astype(BF16)


def lower_mask(rows):
    row_ids = lax.broadcasted_iota(jnp.int32, (rows, rows), 0)
    col_ids = lax.broadcasted_iota(jnp.int32, (rows, rows), 1)
    return row_ids >= col_ids


def span(h):
    return slice(h * DH, (h + 1) * DH)


def states_kernel(pos, k_ref, v_ref, out_ref):
    for h in range(QUAD):
        out_ref[h] = mm(k_ref[:, span(h)], v_ref[:, span(h)], TN)


def forward_kernel(pos, q_ref, k_ref, v_ref, gain_ref, prefix_ref, heads_ref, attn_ref):
    mask = lower_mask(q_ref.shape[0])
    for h in range(QUAD):
        cols = span(h)
        q = q_ref[:, cols]
        scores = jnp.where(mask, mm(q, k_ref[:, cols], NT), 0.0)
        high, low = two_terms(scores)
        top, rest = two_terms(prefix_ref[h])
        v = v_ref[:, cols]
        attn = mm(high, v, NN) + mm(low, v, NN) + mm(q, top, NN) + mm(q, rest, NN)
        rnorm = lax.rsqrt(jnp.mean(attn * attn, axis=-1, keepdims=True) + 1e-06)
        attn_ref[:, cols] = attn
        heads_ref[:, cols] = (attn * rnorm * gain_ref[:, cols]).astype(BF16)


def norm_kernel(pos, q_ref, gain_ref, attn_ref, mine_ref, one_ref, two_ref, three_ref, *refs):
    g_ref, own_ref = refs[-2:]
    for h in range(PAIR):
        cols = span(h)
        attn = attn_ref[:, cols]
        rnorm = lax.rsqrt(jnp.mean(attn * attn, axis=-1, keepdims=True) + 1e-06)
        normed = attn * rnorm
        grads = mine_ref[:, cols]
        for ref in (one_ref, two_ref, three_ref):
            grads = grads + ref[:, cols].astype(F32)
        scaled = grads * gain_ref[:, cols]
        shared = jnp.mean(scaled * normed, axis=-1, keepdims=True)
        g = rnorm * (scaled - normed * shared)
        g_ref[:, cols] = g
        high, low = two_terms(g)
        q = q_ref[:, cols]
        own_ref[h] = mm(q, high, TN) + mm(q, low, TN)


def inner_kernel(pos, q_ref, k_ref, v_ref, g_ref, first_ref, second_ref, *refs):
    gq_ref, gk_ref, gv_ref = refs[-3:]
    mask = lower_mask(q_ref.shape[0])
    for h in range(PAIR):
        cols = span(h)
        q, k, v = q_ref[:, cols], k_ref[:, cols], v_ref[:, cols]
        high, low = two_terms(g_ref[:, cols])
        top, rest = two_terms((first_ref, second_ref)[h][0])
        weights = jnp.where(mask, mm(high, v, NT) + mm(low, v, NT), 0.0).astype(BF16)
        scores = jnp.where(mask, mm(q, k, NT), 0.0).astype(BF16)
        across = mm(high, top, NT) + mm(high, rest, NT) + mm(low, top, NT)
        gq_ref[:, cols] = (across + mm(weights, k, NN)).astype(BF16)
        gk_ref[:, cols] = mm(weights, q, TN)
        gv_ref[:, cols] = mm(scores, high, TN)


def outer_kernel(pos, k_ref, v_ref, gk_ref, gv_ref, first_ref, second_ref, *refs):
    gk_out, gv_out = refs[-2:]
    for h in range(PAIR):
        cols = span(h)
        top, rest = two_terms((first_ref, second_ref)[h][0])
        v, k = v_ref[:, cols], k_ref[:, cols]
        gk_out[:, cols] = (gk_ref[:, cols] + mm(v, top, NT) + mm(v, rest, NT)).astype(BF16)
        gv_out[:, cols] = (gv_ref[:, cols] + mm(k, top, NN) + mm(k, rest, NN)).astype(BF16)


def by_heads(kernel, pos, ins, outs, flops, chunk=None, onto=(), after=()):
    rows = ins[0][0].shape[0]
    count = QUAD if chunk is None else PAIR
    width = count * DH
    each = PLANE if chunk is None else len(chunk)
    steps = PLANE if chunk is None else 2 * each

    def pair_of(s):
        return s if chunk is None else (s // each) * PLANE + chunk[0] + s % each

    def held(head, share, pos):
        return (((head // share) ^ pos[0]) * share + head % share, 0, 0)

    one = (1, DH, DH)
    specs = {
        "cols": pl.BlockSpec((rows, width), lambda s, pos: (0, pair_of(s))),
        "row": pl.BlockSpec((1, width), lambda s, pos: (0, pair_of(s))),
        "chunk": pl.BlockSpec((rows, width), lambda s, pos: (0, s)),
        "own": pl.BlockSpec((count, DH, DH), lambda s, pos: (s, 0, 0)),
        "xor": pl.BlockSpec((count, DH, DH), lambda s, pos: (s ^ pos[0], 0, 0)),
        "prefix0": pl.BlockSpec(one, lambda s, pos: held(pair_of(s) * PAIR, QUAD, pos)),
        "prefix1": pl.BlockSpec(one, lambda s, pos: held(pair_of(s) * PAIR + 1, QUAD, pos)),
        "later0": pl.BlockSpec(one, lambda s, pos: held(s * PAIR, each, pos)),
        "later1": pl.BlockSpec(one, lambda s, pos: held(s * PAIR + 1, each, pos)),
    }
    moved = sum(math.prod(shape) * jnp.dtype(dtype).itemsize for shape, dtype, _ in outs)
    moved += sum(a.size * a.dtype.itemsize for a, _ in ins)
    aliases = {1 + len(ins) + n: at for n, (_, at) in enumerate(onto)}
    unread = [a for a, _ in onto] + list(after)
    return pl.pallas_call(
        kernel,
        grid_spec=pltpu.PrefetchScalarGridSpec(
            num_scalar_prefetch=1,
            grid=(steps,),
            in_specs=[specs[kind] for _, kind in ins] + [pl.BlockSpec(memory_space=pl.ANY)] * len(unread),
            out_specs=[specs[kind] for _, _, kind in outs],
        ),
        out_shape=[jax.ShapeDtypeStruct(shape, dtype) for shape, dtype, _ in outs],
        input_output_aliases=aliases,
        compiler_params=pltpu.CompilerParams(vmem_limit_bytes=24 * MIB),
        cost_estimate=LIGHT,
    )(pos, *[a for a, _ in ins], *unread)


def others_kernel(pos, cot_ref, w_ref, *refs):
    out_ref = refs[-1]
    for t in range(PLANE):
        out_ref[t] = mm(cot_ref[t], w_ref[0], NT).astype(BF16)


def mine_kernel(pos, cot_ref, w_ref, other_ref, *refs):
    own_ref, sent = refs[-4], refs[-3:]
    for t in range(PLANE):
        total = mm(cot_ref[t], w_ref[0], NT) + other_ref[t].astype(F32)
        if t == 0:
            own_ref[...] = total
        else:
            sent[t - 1][...] = total.astype(BF16)


def partial_grads(pos, cot, weights, taken=None, after=()):
    planes, rows, width = weights.shape
    blocks, tokens, _ = cot.shape
    each = planes // 2
    whole = (blocks, tokens, each * rows)
    block = pl.BlockSpec((blocks, tokens, rows), lambda i, pos: (0, 0, i))
    flat = pl.BlockSpec((tokens, rows), lambda i, pos: (0, i))

    def plane_of(i, pos):
        return ((1 - pos[2] if taken is None else pos[2]) * each + i, 0, 0)

    in_specs = [pl.BlockSpec(cot.shape, lambda i, pos: (0, 0, 0)), pl.BlockSpec((1, rows, width), plane_of)]
    if taken is None:
        kernel, out_specs, out_shape, given = others_kernel, block, jax.ShapeDtypeStruct(whole, BF16), ()
    else:
        kernel, given = mine_kernel, (taken,)
        in_specs.append(block)
        out_specs = [flat] * blocks
        out_shape = [jax.ShapeDtypeStruct(whole[1:], F32)] + [jax.ShapeDtypeStruct(whole[1:], BF16)] * (blocks - 1)
    in_specs += [pl.BlockSpec(memory_space=pl.ANY)] * len(after)
    return pl.pallas_call(
        kernel,
        grid_spec=pltpu.PrefetchScalarGridSpec(
            num_scalar_prefetch=1, grid=(each,), in_specs=in_specs, out_specs=out_specs
        ),
        out_shape=out_shape,
        compiler_params=pltpu.CompilerParams(vmem_limit_bytes=40 * MIB),
        cost_estimate=LIGHT,
    )(pos, cot, weights, *given, *after)


def place_kernel(pos, *refs):
    pieces, outs = refs[:PLANE], refs[PLANE:]
    rows = pieces[0].shape[0]
    for k, piece in enumerate(pieces):
        j = pos[0] ^ k
        for chunk, out in zip(CHUNKS, outs, strict=True):

            def store(chunk=chunk, out=out, piece=piece, j=j):
                within = jnp.clip(j - chunk[0], 0, len(chunk) - 1)
                out[pl.ds(pl.multiple_of(within * rows, rows), rows)] = piece[...]

            pl.when((j >= chunk[0]) & (j <= chunk[-1]))(store)


def place_chunks(pos, pieces):
    rows, width = pieces[0].shape
    whole = pl.BlockSpec(memory_space=pltpu.VMEM)
    return pl.pallas_call(
        place_kernel,
        in_specs=[pl.BlockSpec(memory_space=pltpu.SMEM)] + [whole] * len(pieces),
        out_specs=[whole] * len(CHUNKS),
        out_shape=[jax.ShapeDtypeStruct((len(chunk) * rows, width), BF16) for chunk in CHUNKS],
        compiler_params=pltpu.CompilerParams(vmem_limit_bytes=16 * MIB),
        cost_estimate=LIGHT,
    )(pos, *pieces)


def mixed_kernel(pos, *refs):
    groups, weights = (refs[0:5], refs[5:10]), refs[10:12]
    outs, held, sems = refs[-6:-2], refs[-2], refs[-1]
    tokens, width = refs[0].shape
    copies = []
    for group, core in zip(groups, (pos[2], 1 - pos[2]), strict=True):
        columns = pl.ds(pl.multiple_of(core * width, width), width)
        for n, ref in enumerate(group):
            if n < PLANE - 1:
                target = held.at[n, :, columns]
            else:
                count = tokens // 2
                target = held.at[PLANE - 1, pl.ds((n - PLANE + 1) * count, count), columns]
            copy = pltpu.make_async_copy(ref, target, sems.at[len(copies)])
            copy.start()
            copies.append(copy)
    for copy in copies:
        copy.wait()
    planes, rows = weights[0].shape[0], [ref.shape[1] for ref in weights]
    for t in range(PLANE):

        def add(i, total, t=t):
            start = 0
            for ref, count in zip(weights, rows, strict=True):
                at = pl.multiple_of(i * sum(rows) + start, math.gcd(*rows))
                total = total + mm(held[t, :, pl.ds(at, count)], ref[i], NN)
                start += count
            return total

        outs[t][...] = lax.fori_loop(0, planes, add, jnp.zeros(outs[t].shape, F32)).astype(BF16)


def mixed_blocks(pos, x_own, x_other, weights, after):
    tokens, depth = x_own[0].shape
    width = weights[0].shape[2]
    given = list(x_own) + list(x_other)
    whole = pl.BlockSpec(memory_space=pltpu.VMEM)
    return pl.pallas_call(
        mixed_kernel,
        in_specs=[pl.BlockSpec(memory_space=pltpu.SMEM)]
        + [pl.BlockSpec(memory_space=pl.ANY)] * len(given)
        + [whole] * len(weights)
        + [pl.BlockSpec(memory_space=pl.ANY)] * len(after),
        out_specs=[whole] * PLANE,
        out_shape=[jax.ShapeDtypeStruct((tokens, width), BF16)] * PLANE,
        scratch_shapes=[
            pltpu.VMEM((PLANE, tokens, 2 * depth), BF16),
            pltpu.SemaphoreType.DMA((len(given),)),
        ],
        compiler_params=pltpu.CompilerParams(vmem_limit_bytes=40 * MIB),
        cost_estimate=LIGHT,
    )(pos, *given, *weights, *after)


def plane_swap(value, k):
    return lax.ppermute(value, "ctx", [(i, i ^ k) for i in range(PLANE * PLANES)])


def core_swap(value):
    return lax.ppermute(value, "tp", [(0, 1), (1, 0)])


def z_shift(value, by):
    count = PLANE * PLANES
    pairs = [(i, i + by * PLANE) for i in range(count) if 0 <= i + by * PLANE < count]
    return lax.ppermute(value, "ctx", pairs)


def z_gather(value):
    lines = [[z * PLANE + j for z in range(PLANES)] for j in range(PLANE)]
    return lax.all_gather(value, "ctx", axis_index_groups=lines)


def add_kernel(*refs):
    refs[-1][...] = refs[0][...] + refs[1][...]


def add_after(one, two, after):
    whole = pl.BlockSpec(memory_space=pltpu.VMEM)
    return pl.pallas_call(
        add_kernel,
        in_specs=[whole, whole] + [pl.BlockSpec(memory_space=pl.ANY)] * len(after),
        out_specs=whole,
        out_shape=jax.ShapeDtypeStruct(one.shape, one.dtype),
    )(one, two, *after)


def plane_parts(own, p):
    count = own.shape[0] // PLANE
    parts = [lax.dynamic_slice_in_dim(own, (p ^ k) * count, count, 0) for k in range(PLANE)]
    parts = [parts[0]] + [plane_swap(parts[k], k) for k in range(1, PLANE)]
    return parts, parts[0] + parts[1] + parts[2] + parts[3]


def plane_sums(total, backward, after=()):
    sign = -1 if backward else 1
    near = z_shift(total, sign)
    return near + z_shift(add_after(total, near, after) if after else total + near, 2 * sign)


def plane_returns(parts, entering, p, backward):
    given = []
    for t in range(PLANE):
        value = entering
        for k in range(PLANE):
            if k != t:
                ahead = (p ^ k) > (p ^ t) if backward else (p ^ k) < (p ^ t)
                value = value + jnp.where(ahead, parts[k], 0.0)
        given.append(value)
    back = [given[0]] + [plane_swap(given[k], k) for k in range(1, PLANE)]
    return jnp.concatenate(back, axis=0)


def plane_local(queries, keys, values, gain, out_weight, cotangent):
    rows, columns = queries.shape
    heads = columns // DH
    at = lax.axis_index("ctx")
    p, z = at % PLANE, at // PLANE
    pos = jnp.stack([p, z, lax.axis_index("tp")]).astype(jnp.int32)
    wide = out_weight.shape[1] // PLANE

    def quarters(array):
        cut = [lax.dynamic_slice_in_dim(array, (p ^ k) * wide, wide, 1) for k in range(PLANE)]
        return [cut[0]] + [plane_swap(cut[k], k) for k in range(1, PLANE)]

    lined = place_chunks(pos, quarters(out_weight))
    weights = [z_gather(chunk) for chunk in lined]
    cot_pieces = quarters(cotangent)

    (own_state,) = by_heads(
        states_kernel, pos, [(keys, "cols"), (values, "cols")], [((heads, DH, DH), F32, "own")], 2 * rows * columns * DH
    )
    parts, total = plane_parts(own_state, p)
    prefix = plane_returns(parts, plane_sums(total, False, cot_pieces[1:]), p, False)
    gain_row = gain.reshape(1, columns)
    heads_out, attn = by_heads(
        forward_kernel,
        pos,
        [(queries, "cols"), (keys, "cols"), (values, "cols"), (gain_row, "row"), (prefix, "xor")],
        [((rows, columns), BF16, "cols"), ((rows, columns), F32, "cols")],
        2 * rows * columns * (3 * rows + 2 * DH),
    )
    x_one, x_two = plane_swap(heads_out, 1), plane_swap(heads_out, 2)
    x_three = plane_swap(x_one[: rows // 2], 2), plane_swap(x_two[rows // 2 :], 1)
    x_own = [heads_out, x_one, x_two, *x_three]
    x_other = [core_swap(x) for x in x_own]
    cot = jnp.stack(cot_pieces)

    grad_q = grad_k = grad_v = None
    before_others, before_mine = (heads_out,), (x_one, x_two)
    waiting = [(), (*x_three, *x_other)]
    states = []
    for n, (chunk, weight) in enumerate(zip(CHUNKS, weights, strict=True)):
        last = n == len(CHUNKS) - 1
        count = 2 * PAIR * len(chunk)
        part = (rows, count * DH)
        other = core_swap(partial_grads(pos, cot, weight, after=before_others))
        mine, *sent = partial_grads(pos, cot, weight, other, (*before_mine, *waiting[n]))
        blocks = mixed_blocks(pos, x_own, x_other, weights, (sent[0],)) if last else ()
        taken = [plane_swap(sent[k - 1], k) for k in range(1, PLANE)]
        g, own_grad = by_heads(
            norm_kernel,
            pos,
            [(queries, "cols"), (gain_row, "row"), (attn, "cols"), (mine, "chunk")]
            + [(value, "chunk") for value in taken],
            [(part, F32, "chunk"), ((count, DH, DH), F32, "own")],
            0,
            chunk,
            after=blocks[:1],
        )
        parts, total = plane_parts(own_grad, p)
        before_others, before_mine = (own_grad,), (total,)
        states.append((part, g, parts, total))
    for chunk, (part, g, parts, total) in zip(CHUNKS, states, strict=True):
        later = plane_returns(parts, plane_sums(total, True), p, True)
        grad_q, inner_k, inner_v = by_heads(
            inner_kernel,
            pos,
            [(queries, "cols"), (keys, "cols"), (values, "cols"), (g, "chunk"), (prefix, "prefix0"), (prefix, "prefix1")],
            [((rows, columns), BF16, "cols"), (part, F32, "chunk"), (part, F32, "chunk")],
            0,
            chunk,
            [] if grad_q is None else [(grad_q, 0)],
        )
        grad_k, grad_v = by_heads(
            outer_kernel,
            pos,
            [(keys, "cols"), (values, "cols"), (inner_k, "chunk"), (inner_v, "chunk"), (later, "later0"), (later, "later1")],
            [((rows, columns), BF16, "cols"), ((rows, columns), BF16, "cols")],
            0,
            chunk,
            [] if grad_k is None else [(grad_k, 0), (grad_v, 1)],
        )
    mixed = jnp.zeros((rows, PLANE * wide), BF16)
    for k in range(PLANE):
        block = blocks[0] if k == 0 else plane_swap(blocks[k], k)
        mixed = lax.dynamic_update_slice_in_dim(mixed, block, (p ^ k) * wide, 1)
    return mixed, grad_q, grad_k, grad_v


def planes_fit(mesh):
    return mesh.shape["ctx"] == PLANE * PLANES and mesh.shape["tp"] == 2


def solution(mesh):
    placed = (
        P("ctx", "tp"),
        P("ctx", "tp"),
        P("ctx", "tp"),
        P("tp"),
        P("ctx", "tp"),
        P("ctx", "tp"),
    )
    return jax.shard_map(
        plane_local if planes_fit(mesh) else local,
        mesh=mesh,
        in_specs=placed,
        out_specs=(P("ctx", "tp"), P("ctx", "tp"), P("ctx", "tp"), P("ctx", "tp")),
        check_vma=False,
    )
```

```python
import functools
import math

import jax
import jax.numpy as jnp
from jax import lax
from jax.experimental import pallas as pl
from jax.experimental.pallas import tpu as pltpu
from jax.sharding import PartitionSpec as P

DH = 128
F32 = jnp.float32
BF16 = jnp.bfloat16
PLANE = 4
PLANES = 4
CHUNKS = ((0, 1), (2, 3))
QUAD = 4
PAIR = 2
MIB = 1024 * 1024
LIGHT = pl.CostEstimate(flops=1, bytes_accessed=1, transcendentals=0)
NT = (((1,), (1,)), ((), ()))
TN = (((0,), (0,)), ((), ()))
NN = (((1,), (0,)), ((), ()))


def entering(value, axis, join, neutral, backward):
    count, mine = (lax.axis_size(axis), lax.axis_index(axis))
    pieces = lax.all_gather(value, axis)
    if backward:
        pieces = pieces[::-1]
        mine = count - 1 - mine
    running = jnp.full_like(value, 0) + jnp.asarray(neutral, value.dtype)

    def lap(position, running):
        longer = join(running, pieces[position])
        return jnp.where(position < mine, longer, running)

    return lax.fori_loop(0, count - 1, lap, running)


def add_states(earlier, later):
    return earlier + later


def local(queries, keys, values, gain, out_weight, cotangent):
    highest = lax.Precision.HIGHEST
    rows = queries.shape[0]
    heads = queries.shape[1] // DH
    q_heads = queries.reshape(rows, heads, DH)
    k_heads = keys.reshape(rows, heads, DH)
    v_heads = values.reshape(rows, heads, DH)
    q_float = q_heads.astype(jnp.float32)
    k_float = k_heads.astype(jnp.float32)
    v_float = v_heads.astype(jnp.float32)
    row_ids = lax.broadcasted_iota(jnp.int32, (rows, rows), 0)
    col_ids = lax.broadcasted_iota(jnp.int32, (rows, rows), 1)
    mask = (row_ids >= col_ids).astype(jnp.float32)
    zero_state = jnp.zeros((heads, DH, DH), jnp.float32)
    own_state = jnp.einsum("thd,the->hde", k_heads, v_heads, preferred_element_type=jnp.float32)
    prefix = entering(own_state, "ctx", add_states, zero_state, False)
    scores = (
        jnp.einsum("thd,shd->hts", q_heads, k_heads, preferred_element_type=jnp.float32)
        * mask[None]
    )
    attn = jnp.einsum("hts,shd->thd", scores, v_float, precision=highest)
    attn = attn + jnp.einsum("thd,hde->the", q_float, prefix, precision=highest)
    gain_heads = gain.reshape(heads, DH)
    rnorm = lax.rsqrt(jnp.mean(attn * attn, axis=-1, keepdims=True) + 1e-06)
    normed = attn * rnorm
    heads_out = (normed * gain_heads[None]).astype(jnp.bfloat16).reshape(rows, heads * DH)
    weight_all = lax.all_gather(out_weight, "ctx", axis=0, tiled=True)
    mixed = jnp.dot(
        lax.all_gather(heads_out, "tp", axis=1, tiled=True),
        weight_all,
        preferred_element_type=jnp.float32,
    ).astype(jnp.bfloat16)
    partial_grads = lax.dot_general(
        cotangent, weight_all, (((1,), (1,)), ((), ())), preferred_element_type=jnp.float32
    )
    grad_heads = lax.psum_scatter(partial_grads, "tp", scatter_dimension=1, tiled=True).reshape(
        rows, heads, DH
    )
    scaled = grad_heads * gain_heads[None]
    grad_attn = rnorm * (scaled - normed * jnp.mean(scaled * normed, axis=-1, keepdims=True))
    own_grad = jnp.einsum("thd,the->hde", q_float, grad_attn, precision=highest)
    later = entering(own_grad, "ctx", add_states, zero_state, True)
    weights = jnp.einsum("the,she->hts", grad_attn, v_float, precision=highest) * mask[None]
    grad_q = jnp.einsum("the,hde->thd", grad_attn, prefix, precision=highest)
    grad_q = grad_q + jnp.einsum("hts,shd->thd", weights, k_float, precision=highest)
    grad_k = jnp.einsum("she,hde->shd", v_float, later, precision=highest)
    grad_k = grad_k + jnp.einsum("hts,thd->shd", weights, q_float, precision=highest)
    grad_v = jnp.einsum("shd,hde->she", k_float, later, precision=highest)
    grad_v = grad_v + jnp.einsum("hts,the->she", scores, grad_attn, precision=highest)
    grad_queries = grad_q.reshape(rows, heads * DH).astype(jnp.bfloat16)
    grad_keys = grad_k.reshape(rows, heads * DH).astype(jnp.bfloat16)
    grad_values = grad_v.reshape(rows, heads * DH).astype(jnp.bfloat16)
    return (mixed, grad_queries, grad_keys, grad_values)


def mm(a, b, dims):
    return lax.dot_general(a, b, dims, preferred_element_type=F32)


def two_terms(value):
    high = value.astype(BF16)
    return high, (value - high.astype(F32)).astype(BF16)


def lower_mask(rows):
    row_ids = lax.broadcasted_iota(jnp.int32, (rows, rows), 0)
    col_ids = lax.broadcasted_iota(jnp.int32, (rows, rows), 1)
    return row_ids >= col_ids


def span(h):
    return slice(h * DH, (h + 1) * DH)


def prepare_kernel(pos, k_ref, v_ref, w_ref, *outs):
    states, pieces = outs[:PLANE], outs[PLANE:]
    width = pieces[0].shape[1]
    for n in range(PLANE):
        j = pos[0] ^ n
        pieces[n][...] = w_ref[:, pl.ds(pl.multiple_of(j * width, DH), width)]
        for h in range(QUAD):
            cols = pl.ds(pl.multiple_of((j * QUAD + h) * DH, DH), DH)
            states[n][h] = mm(k_ref[:, cols], v_ref[:, cols], TN)


def prepare(pos, keys, values, out_weight):
    whole = pl.BlockSpec(memory_space=pltpu.VMEM)
    piece = (out_weight.shape[0], out_weight.shape[1] // PLANE)
    out = pl.pallas_call(
        prepare_kernel,
        in_specs=[pl.BlockSpec(memory_space=pltpu.SMEM)] + [whole] * 3,
        out_specs=[whole] * (2 * PLANE),
        out_shape=[jax.ShapeDtypeStruct((QUAD, DH, DH), F32)] * PLANE + [jax.ShapeDtypeStruct(piece, BF16)] * PLANE,
        compiler_params=pltpu.CompilerParams(vmem_limit_bytes=56 * MIB),
        cost_estimate=LIGHT,
    )(pos, keys, values, out_weight)
    return out[:PLANE], out[PLANE:]


def forward_kernel(pos, q_ref, k_ref, v_ref, gain_ref, prefix_ref, heads_ref, attn_ref):
    mask = lower_mask(q_ref.shape[0])
    for h in range(QUAD):
        cols = span(h)
        q = q_ref[:, cols]
        scores = jnp.where(mask, mm(q, k_ref[:, cols], NT), 0.0)
        high, low = two_terms(scores)
        top, rest = two_terms(prefix_ref[h])
        v = v_ref[:, cols]
        attn = mm(high, v, NN) + mm(low, v, NN) + mm(q, top, NN) + mm(q, rest, NN)
        rnorm = lax.rsqrt(jnp.mean(attn * attn, axis=-1, keepdims=True) + 1e-06)
        attn_ref[:, cols] = attn
        heads_ref[:, cols] = (attn * rnorm * gain_ref[:, cols]).astype(BF16)


def norm_kernel(pos, q_ref, gain_ref, attn_ref, mine_ref, one_ref, two_ref, three_ref, *refs):
    g_ref, own_ref = refs[-2:]
    for h in range(PAIR):
        cols = span(h)
        attn = attn_ref[:, cols]
        rnorm = lax.rsqrt(jnp.mean(attn * attn, axis=-1, keepdims=True) + 1e-06)
        normed = attn * rnorm
        grads = mine_ref[:, cols]
        for ref in (one_ref, two_ref, three_ref):
            grads = grads + ref[:, cols].astype(F32)
        scaled = grads * gain_ref[:, cols]
        shared = jnp.mean(scaled * normed, axis=-1, keepdims=True)
        g = rnorm * (scaled - normed * shared)
        g_ref[:, cols] = g
        high, low = two_terms(g)
        q = q_ref[:, cols]
        own_ref[h] = mm(q, high, TN) + mm(q, low, TN)


def inner_kernel(pos, q_ref, k_ref, v_ref, g_ref, first_ref, second_ref, *refs):
    gq_ref, gk_ref, gv_ref = refs[-3:]
    mask = lower_mask(q_ref.shape[0])
    for h in range(PAIR):
        cols = span(h)
        q, k, v = q_ref[:, cols], k_ref[:, cols], v_ref[:, cols]
        high, low = two_terms(g_ref[:, cols])
        top, rest = two_terms((first_ref, second_ref)[h][0])
        weights = jnp.where(mask, mm(high, v, NT) + mm(low, v, NT), 0.0).astype(BF16)
        scores = jnp.where(mask, mm(q, k, NT), 0.0).astype(BF16)
        across = mm(high, top, NT) + mm(high, rest, NT) + mm(low, top, NT)
        gq_ref[:, cols] = (across + mm(weights, k, NN)).astype(BF16)
        gk_ref[:, cols] = mm(weights, q, TN)
        gv_ref[:, cols] = mm(scores, high, TN)


def outer_kernel(pos, k_ref, v_ref, gk_ref, gv_ref, later_ref, *refs):
    gk_out, gv_out = refs[-2:]
    for h in range(PAIR):
        cols = span(h)
        top, rest = two_terms(later_ref[h])
        v, k = v_ref[:, cols], k_ref[:, cols]
        gk_out[:, cols] = (gk_ref[:, cols] + mm(v, top, NT) + mm(v, rest, NT)).astype(BF16)
        gv_out[:, cols] = (gv_ref[:, cols] + mm(k, top, NN) + mm(k, rest, NN)).astype(BF16)


def by_heads(kernel, pos, ins, outs, flops, chunk=None, onto=(), after=()):
    rows = ins[0][0].shape[0]
    count = QUAD if chunk is None else PAIR
    width = count * DH
    each = PLANE if chunk is None else len(chunk)
    steps = PLANE if chunk is None else 2 * each

    def pair_of(s):
        return s if chunk is None else (s // each) * PLANE + chunk[0] + s % each

    def held(head, share, pos):
        return (((head // share) ^ pos[0]) * share + head % share, 0, 0)

    one = (1, DH, DH)
    specs = {
        "cols": pl.BlockSpec((rows, width), lambda s, pos: (0, pair_of(s))),
        "row": pl.BlockSpec((1, width), lambda s, pos: (0, pair_of(s))),
        "chunk": pl.BlockSpec((rows, width), lambda s, pos: (0, s)),
        "own": pl.BlockSpec((count, DH, DH), lambda s, pos: (s, 0, 0)),
        "xor": pl.BlockSpec((count, DH, DH), lambda s, pos: (s ^ pos[0], 0, 0)),
        "prefix0": pl.BlockSpec(one, lambda s, pos: held(pair_of(s) * PAIR, QUAD, pos)),
        "prefix1": pl.BlockSpec(one, lambda s, pos: held(pair_of(s) * PAIR + 1, QUAD, pos)),
        "later": pl.BlockSpec(
            (PAIR, DH, DH), lambda s, pos: ((((s // 4) * 2 + s % 2) ^ pos[0]) * len(CHUNKS) + s % 4 // 2, 0, 0)
        ),
    }
    moved = sum(math.prod(shape) * jnp.dtype(dtype).itemsize for shape, dtype, _ in outs)
    moved += sum(a.size * a.dtype.itemsize for a, _ in ins)
    aliases = {1 + len(ins) + n: at for n, (_, at) in enumerate(onto)}
    unread = [a for a, _ in onto] + list(after)
    return pl.pallas_call(
        kernel,
        grid_spec=pltpu.PrefetchScalarGridSpec(
            num_scalar_prefetch=1,
            grid=(steps,),
            in_specs=[specs[kind] for _, kind in ins] + [pl.BlockSpec(memory_space=pl.ANY)] * len(unread),
            out_specs=[specs[kind] for _, _, kind in outs],
        ),
        out_shape=[jax.ShapeDtypeStruct(shape, dtype) for shape, dtype, _ in outs],
        input_output_aliases=aliases,
        compiler_params=pltpu.CompilerParams(vmem_limit_bytes=56 * MIB),
        cost_estimate=LIGHT,
    )(pos, *[a for a, _ in ins], *unread)


def others_kernel(pos, cot_ref, w_ref, *refs):
    out_ref = refs[-1]
    for t in range(PLANE):
        out_ref[t] = mm(cot_ref[t], w_ref[0], NT).astype(BF16)


def mine_kernel(pos, cot_ref, w_ref, other_ref, *refs):
    own_ref, sent = refs[-4], refs[-3:]
    for t in range(PLANE):
        total = mm(cot_ref[t], w_ref[0], NT) + other_ref[t].astype(F32)
        if t == 0:
            own_ref[...] = total
        else:
            sent[t - 1][...] = total.astype(BF16)


def partial_grads(pos, cot, weights, taken=None, after=()):
    planes, rows, width = weights.shape
    blocks, tokens, _ = cot.shape
    each = planes // 2
    whole = (blocks, tokens, each * rows)
    block = pl.BlockSpec((blocks, tokens, rows), lambda i, pos: (0, 0, i))
    flat = pl.BlockSpec((tokens, rows), lambda i, pos: (0, i))

    def plane_of(i, pos):
        return ((1 - pos[2] if taken is None else pos[2]) * each + i, 0, 0)

    in_specs = [pl.BlockSpec(cot.shape, lambda i, pos: (0, 0, 0)), pl.BlockSpec((1, rows, width), plane_of)]
    if taken is None:
        kernel, out_specs, out_shape, given = others_kernel, block, jax.ShapeDtypeStruct(whole, BF16), ()
    else:
        kernel, given = mine_kernel, (taken,)
        in_specs.append(block)
        out_specs = [flat] * blocks
        out_shape = [jax.ShapeDtypeStruct(whole[1:], F32)] + [jax.ShapeDtypeStruct(whole[1:], BF16)] * (blocks - 1)
    in_specs += [pl.BlockSpec(memory_space=pl.ANY)] * len(after)
    return pl.pallas_call(
        kernel,
        grid_spec=pltpu.PrefetchScalarGridSpec(
            num_scalar_prefetch=1, grid=(each,), in_specs=in_specs, out_specs=out_specs
        ),
        out_shape=out_shape,
        compiler_params=pltpu.CompilerParams(vmem_limit_bytes=56 * MIB),
        cost_estimate=LIGHT,
    )(pos, cot, weights, *given, *after)


def place_kernel(pos, *refs):
    pieces, outs = refs[:PLANE], refs[PLANE:]
    rows = pieces[0].shape[0]
    for k, piece in enumerate(pieces):
        j = pos[0] ^ k
        for chunk, out in zip(CHUNKS, outs, strict=True):

            def store(chunk=chunk, out=out, piece=piece, j=j):
                within = jnp.clip(j - chunk[0], 0, len(chunk) - 1)
                out[pl.ds(pl.multiple_of(within * rows, rows), rows)] = piece[...]

            pl.when((j >= chunk[0]) & (j <= chunk[-1]))(store)


def place_chunks(pos, pieces):
    rows, width = pieces[0].shape
    whole = pl.BlockSpec(memory_space=pltpu.VMEM)
    return pl.pallas_call(
        place_kernel,
        in_specs=[pl.BlockSpec(memory_space=pltpu.SMEM)] + [whole] * len(pieces),
        out_specs=[whole] * len(CHUNKS),
        out_shape=[jax.ShapeDtypeStruct((len(chunk) * rows, width), BF16) for chunk in CHUNKS],
        compiler_params=pltpu.CompilerParams(vmem_limit_bytes=56 * MIB),
        cost_estimate=LIGHT,
    )(pos, *pieces)


def mixed_kernel(pos, *refs):
    groups, weights = (refs[0:5], refs[5:10]), refs[10 : 10 + len(CHUNKS)]
    outs, (held, stacked, x_sems, w_sems) = refs[-8:-4], refs[-4:]
    tokens, width = refs[0].shape
    planes, depth = weights[0].shape[0], sum(ref.shape[1] for ref in weights)
    loads = []
    for i in range(planes):
        start = i * depth
        for ref in weights:
            target = stacked.at[pl.ds(start, ref.shape[1])]
            loads.append(pltpu.make_async_copy(ref.at[i], target, w_sems.at[len(loads)]))
            start += ref.shape[1]
    blocks = [[] for _ in range(PLANE)]
    count = 0
    for group, core in zip(groups, (pos[2], 1 - pos[2]), strict=True):
        columns = pl.ds(pl.multiple_of(core * width, width), width)
        for n, ref in enumerate(group):
            target = held.at[min(n, PLANE - 1), :, columns]
            if n >= PLANE - 1:
                part = tokens // 2
                target = held.at[PLANE - 1, pl.ds((n - PLANE + 1) * part, part), columns]
            blocks[min(n, PLANE - 1)].append(pltpu.make_async_copy(ref, target, x_sems.at[count]))
            count += 1
    for copy in blocks[0] + loads + blocks[1] + blocks[2] + blocks[3]:
        copy.start()
    for copy in loads:
        copy.wait()
    for t in range(PLANE):
        for copy in blocks[t]:
            copy.wait()
        outs[t][...] = mm(held[t], stacked[...], NN).astype(BF16)


def mixed_blocks(pos, x_own, x_other, weights, after):
    tokens, depth = x_own[0].shape
    width = weights[0].shape[2]
    given = [*x_own, *x_other, *weights, *after]
    return pl.pallas_call(
        mixed_kernel,
        in_specs=[pl.BlockSpec(memory_space=pltpu.SMEM)] + [pl.BlockSpec(memory_space=pl.ANY)] * len(given),
        out_specs=[pl.BlockSpec(memory_space=pltpu.VMEM)] * PLANE,
        out_shape=[jax.ShapeDtypeStruct((tokens, width), BF16)] * PLANE,
        scratch_shapes=[
            pltpu.VMEM((PLANE, tokens, 2 * depth), BF16),
            pltpu.VMEM((2 * depth, width), BF16),
            pltpu.SemaphoreType.DMA((2 * len(x_own),)),
            pltpu.SemaphoreType.DMA((PLANES * len(weights),)),
        ],
        compiler_params=pltpu.CompilerParams(vmem_limit_bytes=56 * MIB),
        cost_estimate=LIGHT,
    )(pos, *given)


def plane_swap(value, k):
    return lax.ppermute(value, "ctx", [(i, i ^ k) for i in range(PLANE * PLANES)])


def core_swap(value):
    return lax.ppermute(value, "tp", [(0, 1), (1, 0)])


def z_shift(value, by):
    count = PLANE * PLANES
    pairs = [(i, i + by * PLANE) for i in range(count) if 0 <= i + by * PLANE < count]
    return lax.ppermute(value, "ctx", pairs)


def z_gather(value):
    lines = [[z * PLANE + j for z in range(PLANES)] for j in range(PLANE)]
    return lax.all_gather(value, "ctx", axis_index_groups=lines)


def add_kernel(count, *refs):
    total = refs[0][...]
    for ref in refs[1:count]:
        total = total + ref[...]
    refs[-1][...] = total


def add_after(values, after):
    whole = pl.BlockSpec(memory_space=pltpu.VMEM)
    return pl.pallas_call(
        functools.partial(add_kernel, len(values)),
        in_specs=[whole] * len(values) + [pl.BlockSpec(memory_space=pl.ANY)] * len(after),
        out_specs=whole,
        out_shape=jax.ShapeDtypeStruct(values[0].shape, values[0].dtype),
        compiler_params=pltpu.CompilerParams(vmem_limit_bytes=56 * MIB),
        cost_estimate=LIGHT,
    )(*values, *after)


def plane_swaps(parts):
    return [parts[0]] + [plane_swap(parts[k], k) for k in range(1, PLANE)]


def parts_kernel(pos, *refs):
    owns, outs = refs[: len(CHUNKS)], refs[-PLANE:]
    for k in range(PLANE):
        start = 0
        for own in owns:
            count = own.shape[0] // PLANE
            outs[k][start : start + count] = own[pl.ds((pos[0] ^ k) * count, count)]
            start += count


def plane_parts(owns, pos, after):
    whole = pl.BlockSpec(memory_space=pltpu.VMEM)
    part = (sum(own.shape[0] for own in owns) // PLANE, *owns[0].shape[1:])
    parts = pl.pallas_call(
        parts_kernel,
        in_specs=[pl.BlockSpec(memory_space=pltpu.SMEM)] + [whole] * len(owns),
        out_specs=[whole] * PLANE,
        out_shape=[jax.ShapeDtypeStruct(part, owns[0].dtype)] * PLANE,
        compiler_params=pltpu.CompilerParams(vmem_limit_bytes=56 * MIB),
        cost_estimate=LIGHT,
    )(pos, *owns)
    parts = plane_swaps(parts)
    return parts, add_after(parts, after)


def plane_sums(total, backward, after=()):
    sign = -1 if backward else 1
    near = z_shift(total.astype(BF16), sign).astype(F32)
    return near + z_shift(add_after([total, near], after).astype(BF16), 2 * sign).astype(F32)


def plane_returns(parts, entering, p, backward):
    given = []
    for t in range(PLANE):
        value = entering
        for k in range(PLANE):
            if k != t:
                ahead = (p ^ k) > (p ^ t) if backward else (p ^ k) < (p ^ t)
                value = value + jnp.where(ahead, parts[k], 0.0)
        given.append(value)
    return jnp.concatenate(plane_swaps(given), axis=0)


def plane_local(queries, keys, values, gain, out_weight, cotangent):
    rows, columns = queries.shape
    at = lax.axis_index("ctx")
    p, z = at % PLANE, at // PLANE
    pos = jnp.stack([p, z, lax.axis_index("tp")]).astype(jnp.int32)
    wide = out_weight.shape[1] // PLANE

    states, pieces = prepare(pos, keys, values, out_weight)
    parts = plane_swaps(states)
    total = add_after(parts, ())
    weights = [z_gather(chunk) for chunk in place_chunks(pos, plane_swaps(pieces))]
    cot_pieces = plane_swaps([lax.dynamic_slice_in_dim(cotangent, (p ^ k) * wide, wide, 1) for k in range(PLANE)])
    prefix = plane_returns(parts, plane_sums(total, False, cot_pieces[1:]), p, False)
    cot = jnp.stack(cot_pieces)
    gain_row = gain.reshape(1, columns)
    heads_out, attn = by_heads(
        forward_kernel,
        pos,
        [(queries, "cols"), (keys, "cols"), (values, "cols"), (gain_row, "row"), (prefix, "xor")],
        [((rows, columns), BF16, "cols"), ((rows, columns), F32, "cols")],
        2 * rows * columns * (3 * rows + 2 * DH),
    )
    x_one, x_two = plane_swap(heads_out, 1), plane_swap(heads_out, 2)
    x_three = plane_swap(x_one[: rows // 2], 2), plane_swap(x_two[rows // 2 :], 1)
    x_own = [heads_out, x_one, x_two, *x_three]
    x_other = [core_swap(x) for x in x_own]

    before_others, before_norm = (heads_out,), ()
    before_mine = (x_one, x_two)
    owns, inners = [], []
    for n, (chunk, weight) in enumerate(zip(CHUNKS, weights, strict=True)):
        last = n == len(CHUNKS) - 1
        count = 2 * PAIR * len(chunk)
        if n == 0:
            other = core_swap(partial_grads(pos, cot, weight, after=before_others))
            mine, *sent = partial_grads(pos, cot, weight, other, before_mine)
        else:
            mine, *sent = partial_grads(pos, cot, weight, core_swap(theirs), before_mine)
        if last:
            blocks = mixed_blocks(pos, x_own, x_other, weights, (sent[0],))
            before_norm = (blocks[0], inners[0])
        taken = plane_swaps([None, *sent])[1:]
        if not last:
            theirs = partial_grads(pos, cot, weights[n + 1], after=(*taken, *x_three))
            before_norm = (theirs,)
        g, own_grad = by_heads(
            norm_kernel,
            pos,
            [(queries, "cols"), (gain_row, "row"), (attn, "cols"), (mine, "chunk")]
            + [(value, "chunk") for value in taken],
            [((rows, count * DH), F32, "chunk"), ((count, DH, DH), F32, "own")],
            0,
            chunk,
            after=before_norm,
        )
        before_mine = (own_grad,)
        owns.append(own_grad)
        inners = by_heads(
            inner_kernel,
            pos,
            [(queries, "cols"), (keys, "cols"), (values, "cols"), (g, "chunk"), (prefix, "prefix0"), (prefix, "prefix1")],
            [((rows, columns), BF16, "cols"), ((rows, columns), F32, "cols"), ((rows, columns), F32, "cols")],
            0,
            chunk,
            list(zip(inners, range(3), strict=False)),
        )
    grad_q, inner_k, inner_v = inners
    parts, total = plane_parts(owns, pos, ())
    later = plane_returns(parts, plane_sums(total, True, (grad_q,)), p, True)
    grad_k, grad_v = by_heads(
        outer_kernel,
        pos,
        [(keys, "cols"), (values, "cols"), (inner_k, "cols"), (inner_v, "cols"), (later, "later")],
        [((rows, columns), BF16, "cols"), ((rows, columns), BF16, "cols")],
        0,
        (0, 1, 2, 3),
    )
    mixed = jnp.zeros((rows, PLANE * wide), BF16)
    for k in range(PLANE):
        block = blocks[0] if k == 0 else plane_swap(blocks[k], k)
        mixed = lax.dynamic_update_slice_in_dim(mixed, block, (p ^ k) * wide, 1)
    return mixed, grad_q, grad_k, grad_v


def planes_fit(mesh):
    return mesh.shape["ctx"] == PLANE * PLANES and mesh.shape["tp"] == 2


def solution(mesh):
    placed = (
        P("ctx", "tp"),
        P("ctx", "tp"),
        P("ctx", "tp"),
        P("tp"),
        P("ctx", "tp"),
        P("ctx", "tp"),
    )
    return jax.shard_map(
        plane_local if planes_fit(mesh) else local,
        mesh=mesh,
        in_specs=placed,
        out_specs=(P("ctx", "tp"), P("ctx", "tp"), P("ctx", "tp"), P("ctx", "tp")),
        check_vma=False,
    )
```

```python
import functools
import math

import jax
import jax.numpy as jnp
from jax import lax
from jax.experimental import pallas as pl
from jax.experimental.pallas import tpu as pltpu
from jax.sharding import PartitionSpec as P

DH = 128
F32 = jnp.float32
BF16 = jnp.bfloat16
PLANE = 4
PLANES = 4
CHUNKS = ((0, 1), (2, 3))
QUAD = 4
PAIR = 2
MIB = 1024 * 1024
LIGHT = pl.CostEstimate(flops=1, bytes_accessed=1, transcendentals=0)
NT = (((1,), (1,)), ((), ()))
TN = (((0,), (0,)), ((), ()))
NN = (((1,), (0,)), ((), ()))


def entering(value, axis, join, neutral, backward):
    count, mine = (lax.axis_size(axis), lax.axis_index(axis))
    pieces = lax.all_gather(value, axis)
    if backward:
        pieces = pieces[::-1]
        mine = count - 1 - mine
    running = jnp.full_like(value, 0) + jnp.asarray(neutral, value.dtype)

    def lap(position, running):
        longer = join(running, pieces[position])
        return jnp.where(position < mine, longer, running)

    return lax.fori_loop(0, count - 1, lap, running)


def add_states(earlier, later):
    return earlier + later


def local(queries, keys, values, gain, out_weight, cotangent):
    highest = lax.Precision.HIGHEST
    rows = queries.shape[0]
    heads = queries.shape[1] // DH
    q_heads = queries.reshape(rows, heads, DH)
    k_heads = keys.reshape(rows, heads, DH)
    v_heads = values.reshape(rows, heads, DH)
    q_float = q_heads.astype(jnp.float32)
    k_float = k_heads.astype(jnp.float32)
    v_float = v_heads.astype(jnp.float32)
    row_ids = lax.broadcasted_iota(jnp.int32, (rows, rows), 0)
    col_ids = lax.broadcasted_iota(jnp.int32, (rows, rows), 1)
    mask = (row_ids >= col_ids).astype(jnp.float32)
    zero_state = jnp.zeros((heads, DH, DH), jnp.float32)
    own_state = jnp.einsum("thd,the->hde", k_heads, v_heads, preferred_element_type=jnp.float32)
    prefix = entering(own_state, "ctx", add_states, zero_state, False)
    scores = (
        jnp.einsum("thd,shd->hts", q_heads, k_heads, preferred_element_type=jnp.float32)
        * mask[None]
    )
    attn = jnp.einsum("hts,shd->thd", scores, v_float, precision=highest)
    attn = attn + jnp.einsum("thd,hde->the", q_float, prefix, precision=highest)
    gain_heads = gain.reshape(heads, DH)
    rnorm = lax.rsqrt(jnp.mean(attn * attn, axis=-1, keepdims=True) + 1e-06)
    normed = attn * rnorm
    heads_out = (normed * gain_heads[None]).astype(jnp.bfloat16).reshape(rows, heads * DH)
    weight_all = lax.all_gather(out_weight, "ctx", axis=0, tiled=True)
    mixed = jnp.dot(
        lax.all_gather(heads_out, "tp", axis=1, tiled=True),
        weight_all,
        preferred_element_type=jnp.float32,
    ).astype(jnp.bfloat16)
    partial_grads = lax.dot_general(
        cotangent, weight_all, (((1,), (1,)), ((), ())), preferred_element_type=jnp.float32
    )
    grad_heads = lax.psum_scatter(partial_grads, "tp", scatter_dimension=1, tiled=True).reshape(
        rows, heads, DH
    )
    scaled = grad_heads * gain_heads[None]
    grad_attn = rnorm * (scaled - normed * jnp.mean(scaled * normed, axis=-1, keepdims=True))
    own_grad = jnp.einsum("thd,the->hde", q_float, grad_attn, precision=highest)
    later = entering(own_grad, "ctx", add_states, zero_state, True)
    weights = jnp.einsum("the,she->hts", grad_attn, v_float, precision=highest) * mask[None]
    grad_q = jnp.einsum("the,hde->thd", grad_attn, prefix, precision=highest)
    grad_q = grad_q + jnp.einsum("hts,shd->thd", weights, k_float, precision=highest)
    grad_k = jnp.einsum("she,hde->shd", v_float, later, precision=highest)
    grad_k = grad_k + jnp.einsum("hts,thd->shd", weights, q_float, precision=highest)
    grad_v = jnp.einsum("shd,hde->she", k_float, later, precision=highest)
    grad_v = grad_v + jnp.einsum("hts,the->she", scores, grad_attn, precision=highest)
    grad_queries = grad_q.reshape(rows, heads * DH).astype(jnp.bfloat16)
    grad_keys = grad_k.reshape(rows, heads * DH).astype(jnp.bfloat16)
    grad_values = grad_v.reshape(rows, heads * DH).astype(jnp.bfloat16)
    return (mixed, grad_queries, grad_keys, grad_values)


def mm(a, b, dims):
    return lax.dot_general(a, b, dims, preferred_element_type=F32)


def two_terms(value):
    high = value.astype(BF16)
    return high, (value - high.astype(F32)).astype(BF16)


def lower_mask(rows):
    row_ids = lax.broadcasted_iota(jnp.int32, (rows, rows), 0)
    col_ids = lax.broadcasted_iota(jnp.int32, (rows, rows), 1)
    return row_ids >= col_ids


def span(h):
    return slice(h * DH, (h + 1) * DH)


def pieces_kernel(pos, w_ref, *outs):
    width = outs[0].shape[1]
    for n in range(PLANE):
        outs[n][...] = w_ref[:, pl.ds(pl.multiple_of((pos[0] ^ n) * width, DH), width)]


def states_kernel(pos, k_ref, v_ref, *refs):
    for n in range(PLANE):
        for h in range(QUAD):
            cols = pl.ds(pl.multiple_of(((pos[0] ^ n) * QUAD + h) * DH, DH), DH)
            refs[n - PLANE][h] = mm(k_ref[:, cols], v_ref[:, cols], TN)


def prepare(pos, keys, values, out_weight):
    whole = pl.BlockSpec(memory_space=pltpu.VMEM)
    place = pl.BlockSpec(memory_space=pltpu.SMEM)
    piece = (out_weight.shape[0], out_weight.shape[1] // PLANE)
    params = pltpu.CompilerParams(vmem_limit_bytes=56 * MIB)
    pieces = pl.pallas_call(
        pieces_kernel,
        in_specs=[place, whole],
        out_specs=[whole] * PLANE,
        out_shape=[jax.ShapeDtypeStruct(piece, BF16)] * PLANE,
        compiler_params=params,
        cost_estimate=LIGHT,
    )(pos, out_weight)
    states = pl.pallas_call(
        states_kernel,
        in_specs=[place, whole, whole, pl.BlockSpec(memory_space=pl.ANY)],
        out_specs=[whole] * PLANE,
        out_shape=[jax.ShapeDtypeStruct((QUAD, DH, DH), F32)] * PLANE,
        compiler_params=params,
        cost_estimate=LIGHT,
    )(pos, keys, values, pieces[0])
    return states, pieces


def forward_kernel(pos, q_ref, k_ref, v_ref, gain_ref, prefix_ref, heads_ref, attn_ref):
    mask = lower_mask(q_ref.shape[0])
    for h in range(QUAD):
        cols = span(h)
        q = q_ref[:, cols]
        scores = jnp.where(mask, mm(q, k_ref[:, cols], NT), 0.0)
        high, low = two_terms(scores)
        top, rest = two_terms(prefix_ref[h])
        v = v_ref[:, cols]
        attn = mm(high, v, NN) + mm(low, v, NN) + mm(q, top, NN) + mm(q, rest, NN)
        rnorm = lax.rsqrt(jnp.mean(attn * attn, axis=-1, keepdims=True) + 1e-06)
        attn_ref[:, cols] = attn
        heads_ref[:, cols] = (attn * rnorm * gain_ref[:, cols]).astype(BF16)


def norm_kernel(pos, q_ref, gain_ref, attn_ref, mine_ref, one_ref, two_ref, three_ref, *refs):
    g_ref, own_ref = refs[-2:]
    for h in range(PAIR):
        cols = span(h)
        attn = attn_ref[:, cols]
        rnorm = lax.rsqrt(jnp.mean(attn * attn, axis=-1, keepdims=True) + 1e-06)
        normed = attn * rnorm
        grads = mine_ref[:, cols]
        for ref in (one_ref, two_ref, three_ref):
            grads = grads + ref[:, cols].astype(F32)
        scaled = grads * gain_ref[:, cols]
        shared = jnp.mean(scaled * normed, axis=-1, keepdims=True)
        g = rnorm * (scaled - normed * shared)
        g_ref[:, cols] = g
        high, low = two_terms(g)
        q = q_ref[:, cols]
        own_ref[h] = mm(q, high, TN) + mm(q, low, TN)


def inner_kernel(pos, q_ref, k_ref, v_ref, g_ref, first_ref, second_ref, *refs):
    gq_ref, gk_ref, gv_ref = refs[-3:]
    mask = lower_mask(q_ref.shape[0])
    for h in range(PAIR):
        cols = span(h)
        q, k, v = q_ref[:, cols], k_ref[:, cols], v_ref[:, cols]
        high, low = two_terms(g_ref[:, cols])
        top, rest = two_terms((first_ref, second_ref)[h][0])
        weights = jnp.where(mask, mm(high, v, NT) + mm(low, v, NT), 0.0).astype(BF16)
        scores = jnp.where(mask, mm(q, k, NT), 0.0).astype(BF16)
        across = mm(high, top, NT) + mm(high, rest, NT) + mm(low, top, NT)
        gq_ref[:, cols] = (across + mm(weights, k, NN)).astype(BF16)
        gk_ref[:, cols] = mm(weights, q, TN)
        gv_ref[:, cols] = mm(scores, high, TN)


def outer_kernel(pos, k_ref, v_ref, gk_ref, gv_ref, later_ref, *refs):
    gk_out, gv_out = refs[-2:]
    for h in range(PAIR):
        cols = span(h)
        top, rest = two_terms(later_ref[h])
        v, k = v_ref[:, cols], k_ref[:, cols]
        gk_out[:, cols] = (gk_ref[:, cols] + mm(v, top, NT) + mm(v, rest, NT)).astype(BF16)
        gv_out[:, cols] = (gv_ref[:, cols] + mm(k, top, NN) + mm(k, rest, NN)).astype(BF16)


def by_heads(kernel, pos, ins, outs, flops, chunk=None, onto=(), after=()):
    rows = ins[0][0].shape[0]
    count = QUAD if chunk is None else PAIR
    width = count * DH
    each = PLANE if chunk is None else len(chunk)
    steps = PLANE if chunk is None else 2 * each

    def pair_of(s):
        return s if chunk is None else (s // each) * PLANE + chunk[0] + s % each

    def held(head, share, pos):
        return (((head // share) ^ pos[0]) * share + head % share, 0, 0)

    one = (1, DH, DH)
    specs = {
        "cols": pl.BlockSpec((rows, width), lambda s, pos: (0, pair_of(s))),
        "row": pl.BlockSpec((1, width), lambda s, pos: (0, pair_of(s))),
        "chunk": pl.BlockSpec((rows, width), lambda s, pos: (0, s)),
        "own": pl.BlockSpec((count, DH, DH), lambda s, pos: (s, 0, 0)),
        "xor": pl.BlockSpec((count, DH, DH), lambda s, pos: (s ^ pos[0], 0, 0)),
        "prefix0": pl.BlockSpec(one, lambda s, pos: held(pair_of(s) * PAIR, QUAD, pos)),
        "prefix1": pl.BlockSpec(one, lambda s, pos: held(pair_of(s) * PAIR + 1, QUAD, pos)),
        "later": pl.BlockSpec(
            (PAIR, DH, DH), lambda s, pos: ((((s // 4) * 2 + s % 2) ^ pos[0]) * len(CHUNKS) + s % 4 // 2, 0, 0)
        ),
    }
    moved = sum(math.prod(shape) * jnp.dtype(dtype).itemsize for shape, dtype, _ in outs)
    moved += sum(a.size * a.dtype.itemsize for a, _ in ins)
    aliases = {1 + len(ins) + n: at for n, (_, at) in enumerate(onto)}
    unread = [a for a, _ in onto] + list(after)
    return pl.pallas_call(
        kernel,
        grid_spec=pltpu.PrefetchScalarGridSpec(
            num_scalar_prefetch=1,
            grid=(steps,),
            in_specs=[specs[kind] for _, kind in ins] + [pl.BlockSpec(memory_space=pl.ANY)] * len(unread),
            out_specs=[specs[kind] for _, _, kind in outs],
        ),
        out_shape=[jax.ShapeDtypeStruct(shape, dtype) for shape, dtype, _ in outs],
        input_output_aliases=aliases,
        compiler_params=pltpu.CompilerParams(vmem_limit_bytes=56 * MIB),
        cost_estimate=LIGHT,
    )(pos, *[a for a, _ in ins], *unread)


def others_kernel(pos, cot_ref, w_ref, *refs):
    out_ref = refs[-1]
    for t in range(PLANE):
        out_ref[t] = mm(cot_ref[t], w_ref[0], NT)


def mine_kernel(pos, cot_ref, w_ref, other_ref, *refs):
    own_ref, sent = refs[-4], refs[-3:]
    for t in range(PLANE):
        total = mm(cot_ref[t], w_ref[0], NT) + other_ref[t]
        if t == 0:
            own_ref[...] = total
        else:
            sent[t - 1][...] = total.astype(BF16)


def partial_grads(pos, cot, weights, taken=None, after=()):
    planes, rows, width = weights.shape
    blocks, tokens, _ = cot.shape
    each = planes // 2
    whole = (blocks, tokens, each * rows)
    block = pl.BlockSpec((blocks, tokens, rows), lambda i, pos: (0, 0, i))
    flat = pl.BlockSpec((tokens, rows), lambda i, pos: (0, i))

    def plane_of(i, pos):
        return ((1 - pos[2] if taken is None else pos[2]) * each + i, 0, 0)

    in_specs = [pl.BlockSpec(cot.shape, lambda i, pos: (0, 0, 0)), pl.BlockSpec((1, rows, width), plane_of)]
    if taken is None:
        kernel, out_specs, out_shape, given = others_kernel, block, jax.ShapeDtypeStruct(whole, F32), ()
    else:
        kernel, given = mine_kernel, (taken,)
        in_specs.append(block)
        out_specs = [flat] * blocks
        out_shape = [jax.ShapeDtypeStruct(whole[1:], F32)] + [jax.ShapeDtypeStruct(whole[1:], BF16)] * (blocks - 1)
    in_specs += [pl.BlockSpec(memory_space=pl.ANY)] * len(after)
    return pl.pallas_call(
        kernel,
        grid_spec=pltpu.PrefetchScalarGridSpec(
            num_scalar_prefetch=1, grid=(each,), in_specs=in_specs, out_specs=out_specs
        ),
        out_shape=out_shape,
        compiler_params=pltpu.CompilerParams(vmem_limit_bytes=56 * MIB),
        cost_estimate=LIGHT,
    )(pos, cot, weights, *given, *after)


def place_kernel(pos, *refs):
    pieces, outs = refs[:PLANE], refs[-len(CHUNKS) :]
    rows = pieces[0].shape[0]
    for k, piece in enumerate(pieces):
        j = pos[0] ^ k
        for chunk, out in zip(CHUNKS, outs, strict=True):

            def store(chunk=chunk, out=out, piece=piece, j=j):
                within = jnp.clip(j - chunk[0], 0, len(chunk) - 1)
                out[pl.ds(pl.multiple_of(within * rows, rows), rows)] = piece[...]

            pl.when((j >= chunk[0]) & (j <= chunk[-1]))(store)


def place_chunks(pos, pieces, after):
    rows, width = pieces[0].shape
    whole = pl.BlockSpec(memory_space=pltpu.VMEM)
    return pl.pallas_call(
        place_kernel,
        in_specs=[pl.BlockSpec(memory_space=pltpu.SMEM)] + [whole] * len(pieces)
        + [pl.BlockSpec(memory_space=pl.ANY)] * len(after),
        out_specs=[whole] * len(CHUNKS),
        out_shape=[jax.ShapeDtypeStruct((len(chunk) * rows, width), BF16) for chunk in CHUNKS],
        compiler_params=pltpu.CompilerParams(vmem_limit_bytes=56 * MIB),
        cost_estimate=LIGHT,
    )(pos, *pieces, *after)


def mixed_kernel(pos, *refs):
    groups, weights = (refs[0:5], refs[5:10]), refs[10 : 10 + len(CHUNKS)]
    outs, (held, stacked, x_sems, w_sems) = refs[-8:-4], refs[-4:]
    tokens, width = refs[0].shape
    planes, depth = weights[0].shape[0], sum(ref.shape[1] for ref in weights)
    loads = []
    for i in range(planes):
        start = i * depth
        for ref in weights:
            target = stacked.at[pl.ds(start, ref.shape[1])]
            loads.append(pltpu.make_async_copy(ref.at[i], target, w_sems.at[len(loads)]))
            start += ref.shape[1]
    blocks = [[] for _ in range(PLANE)]
    count = 0
    for group, core in zip(groups, (pos[2], 1 - pos[2]), strict=True):
        columns = pl.ds(pl.multiple_of(core * width, width), width)
        for n, ref in enumerate(group):
            target = held.at[min(n, PLANE - 1), :, columns]
            if n >= PLANE - 1:
                part = tokens // 2
                target = held.at[PLANE - 1, pl.ds((n - PLANE + 1) * part, part), columns]
            blocks[min(n, PLANE - 1)].append(pltpu.make_async_copy(ref, target, x_sems.at[count]))
            count += 1
    for copy in blocks[0] + loads + blocks[1] + blocks[2] + blocks[3]:
        copy.start()
    for copy in loads:
        copy.wait()
    for t in range(PLANE):
        for copy in blocks[t]:
            copy.wait()
        outs[t][...] = mm(held[t], stacked[...], NN).astype(BF16)


def mixed_blocks(pos, x_own, x_other, weights, after):
    tokens, depth = x_own[0].shape
    width = weights[0].shape[2]
    given = [*x_own, *x_other, *weights, *after]
    return pl.pallas_call(
        mixed_kernel,
        in_specs=[pl.BlockSpec(memory_space=pltpu.SMEM)] + [pl.BlockSpec(memory_space=pl.ANY)] * len(given),
        out_specs=[pl.BlockSpec(memory_space=pltpu.VMEM)] * PLANE,
        out_shape=[jax.ShapeDtypeStruct((tokens, width), BF16)] * PLANE,
        scratch_shapes=[
            pltpu.VMEM((PLANE, tokens, 2 * depth), BF16),
            pltpu.VMEM((2 * depth, width), BF16),
            pltpu.SemaphoreType.DMA((2 * len(x_own),)),
            pltpu.SemaphoreType.DMA((PLANES * len(weights),)),
        ],
        compiler_params=pltpu.CompilerParams(vmem_limit_bytes=56 * MIB),
        cost_estimate=LIGHT,
    )(pos, *given)


def plane_swap(value, k):
    return lax.ppermute(value, "ctx", [(i, i ^ k) for i in range(PLANE * PLANES)])


def core_swap(value):
    return lax.ppermute(value, "tp", [(0, 1), (1, 0)])


def z_shift(value, by):
    count = PLANE * PLANES
    pairs = [(i, i + by * PLANE) for i in range(count) if 0 <= i + by * PLANE < count]
    return lax.ppermute(value, "ctx", pairs)


def z_gather(value):
    lines = [[z * PLANE + j for z in range(PLANES)] for j in range(PLANE)]
    return lax.all_gather(value, "ctx", axis_index_groups=lines)


def add_kernel(count, *refs):
    total = refs[0][...]
    for ref in refs[1:count]:
        total = total + ref[...]
    refs[-1][...] = total


def add_after(values, after):
    whole = pl.BlockSpec(memory_space=pltpu.VMEM)
    return pl.pallas_call(
        functools.partial(add_kernel, len(values)),
        in_specs=[whole] * len(values) + [pl.BlockSpec(memory_space=pl.ANY)] * len(after),
        out_specs=whole,
        out_shape=jax.ShapeDtypeStruct(values[0].shape, F32),
        compiler_params=pltpu.CompilerParams(vmem_limit_bytes=56 * MIB),
        cost_estimate=LIGHT,
    )(*values, *after)


def plane_swaps(parts):
    return [parts[0]] + [plane_swap(parts[k], k) for k in range(1, PLANE)]


def parts_kernel(pos, *refs):
    owns, outs = refs[: len(CHUNKS)], refs[-PLANE:]
    for k in range(PLANE):
        start = 0
        for own in owns:
            count = own.shape[0] // PLANE
            outs[k][start : start + count] = own[pl.ds((pos[0] ^ k) * count, count)]
            start += count


def plane_parts(owns, pos, after):
    whole = pl.BlockSpec(memory_space=pltpu.VMEM)
    part = (sum(own.shape[0] for own in owns) // PLANE, *owns[0].shape[1:])
    parts = pl.pallas_call(
        parts_kernel,
        in_specs=[pl.BlockSpec(memory_space=pltpu.SMEM)] + [whole] * len(owns),
        out_specs=[whole] * PLANE,
        out_shape=[jax.ShapeDtypeStruct(part, owns[0].dtype)] * PLANE,
        compiler_params=pltpu.CompilerParams(vmem_limit_bytes=56 * MIB),
        cost_estimate=LIGHT,
    )(pos, *owns)
    parts = plane_swaps(parts)
    return parts, add_after(parts, after)


def plane_sums(total, backward, after=()):
    sign = -1 if backward else 1
    near = z_shift(total, sign)
    return near, z_shift(add_after([total, near], after), 2 * sign)


def returns_kernel(backward, pos, near_ref, far_ref, *refs):
    parts, outs = refs[:PLANE], refs[PLANE:]
    entering = near_ref[...] + far_ref[...]
    for t in range(PLANE):
        value = entering
        for k in range(PLANE):
            if k != t:
                here, there = pos[0] ^ k, pos[0] ^ t
                ahead = here > there if backward else here < there
                value = value + jnp.where(ahead, parts[k][...], 0.0)
        outs[t][...] = value


def plane_returns(pos, parts, sums, backward):
    whole = pl.BlockSpec(memory_space=pltpu.VMEM)
    given = pl.pallas_call(
        functools.partial(returns_kernel, backward),
        in_specs=[pl.BlockSpec(memory_space=pltpu.SMEM)] + [whole] * (2 + PLANE),
        out_specs=[whole] * PLANE,
        out_shape=[jax.ShapeDtypeStruct(parts[0].shape, F32)] * PLANE,
        compiler_params=pltpu.CompilerParams(vmem_limit_bytes=56 * MIB),
        cost_estimate=LIGHT,
    )(pos, *sums, *parts)
    return jnp.concatenate(plane_swaps(given), axis=0)


def plane_local(queries, keys, values, gain, out_weight, cotangent):
    rows, columns = queries.shape
    at = lax.axis_index("ctx")
    p, z = at % PLANE, at // PLANE
    pos = jnp.stack([p, z, lax.axis_index("tp")]).astype(jnp.int32)
    wide = out_weight.shape[1] // PLANE

    states, pieces = prepare(pos, keys, values, out_weight)
    parts = plane_swaps(states)
    total = add_after(parts, ())
    weights = [z_gather(chunk) for chunk in place_chunks(pos, plane_swaps(pieces), (states[0],))]
    cot_pieces = plane_swaps([lax.dynamic_slice_in_dim(cotangent, (p ^ k) * wide, wide, 1) for k in range(PLANE)])
    prefix = plane_returns(pos, parts, plane_sums(total, False, cot_pieces[1:]), False)
    cot = jnp.stack(cot_pieces)
    gain_row = gain.reshape(1, columns)
    heads_out, attn = by_heads(
        forward_kernel,
        pos,
        [(queries, "cols"), (keys, "cols"), (values, "cols"), (gain_row, "row"), (prefix, "xor")],
        [((rows, columns), BF16, "cols"), ((rows, columns), F32, "cols")],
        2 * rows * columns * (3 * rows + 2 * DH),
    )
    x_one, x_two = plane_swap(heads_out, 1), plane_swap(heads_out, 2)
    x_three = plane_swap(x_one[: rows // 2], 2), plane_swap(x_two[rows // 2 :], 1)
    x_own = [heads_out, x_one, x_two, *x_three]
    x_other = [core_swap(x) for x in x_own]

    before_others, before_norm = (heads_out,), ()
    before_mine = (x_one, x_two)
    owns, inners = [], []
    for n, (chunk, weight) in enumerate(zip(CHUNKS, weights, strict=True)):
        last = n == len(CHUNKS) - 1
        count = 2 * PAIR * len(chunk)
        if n == 0:
            other = core_swap(partial_grads(pos, cot, weight, after=before_others))
            mine, *sent = partial_grads(pos, cot, weight, other, before_mine)
        else:
            mine, *sent = partial_grads(pos, cot, weight, core_swap(theirs), before_mine)
        if last:
            blocks = mixed_blocks(pos, x_own, x_other, weights, (sent[0],))
            before_norm = (blocks[0], inners[0])
        taken = plane_swaps([None, *sent])[1:]
        if not last:
            theirs = partial_grads(pos, cot, weights[n + 1], after=(*taken, *x_three))
            before_norm = (theirs,)
        g, own_grad = by_heads(
            norm_kernel,
            pos,
            [(queries, "cols"), (gain_row, "row"), (attn, "cols"), (mine, "chunk")]
            + [(value, "chunk") for value in taken],
            [((rows, count * DH), F32, "chunk"), ((count, DH, DH), F32, "own")],
            0,
            chunk,
            after=before_norm,
        )
        before_mine = (own_grad,)
        owns.append(own_grad)
        inners = by_heads(
            inner_kernel,
            pos,
            [(queries, "cols"), (keys, "cols"), (values, "cols"), (g, "chunk"), (prefix, "prefix0"), (prefix, "prefix1")],
            [((rows, columns), BF16, "cols"), ((rows, columns), F32, "cols"), ((rows, columns), F32, "cols")],
            0,
            chunk,
            list(zip(inners, range(3), strict=False)),
        )
    grad_q, inner_k, inner_v = inners
    parts, total = plane_parts(owns, pos, ())
    later = plane_returns(pos, parts, plane_sums(total, True, (grad_q,)), True)
    grad_k, grad_v = by_heads(
        outer_kernel,
        pos,
        [(keys, "cols"), (values, "cols"), (inner_k, "cols"), (inner_v, "cols"), (later, "later")],
        [((rows, columns), BF16, "cols"), ((rows, columns), BF16, "cols")],
        0,
        (0, 1, 2, 3),
    )
    mixed = jnp.zeros((rows, PLANE * wide), BF16)
    for k in range(PLANE):
        block = blocks[0] if k == 0 else plane_swap(blocks[k], k)
        mixed = lax.dynamic_update_slice_in_dim(mixed, block, (p ^ k) * wide, 1)
    return mixed, grad_q, grad_k, grad_v


def planes_fit(mesh):
    return mesh.shape["ctx"] == PLANE * PLANES and mesh.shape["tp"] == 2


def solution(mesh):
    placed = (
        P("ctx", "tp"),
        P("ctx", "tp"),
        P("ctx", "tp"),
        P("tp"),
        P("ctx", "tp"),
        P("ctx", "tp"),
    )
    return jax.shard_map(
        plane_local if planes_fit(mesh) else local,
        mesh=mesh,
        in_specs=placed,
        out_specs=(P("ctx", "tp"), P("ctx", "tp"), P("ctx", "tp"), P("ctx", "tp")),
        check_vma=False,
    )
```

```python
import functools
import math

import jax
import jax.numpy as jnp
from jax import lax
from jax.experimental import pallas as pl
from jax.experimental.pallas import tpu as pltpu
from jax.sharding import PartitionSpec as P

DH = 128
F32 = jnp.float32
BF16 = jnp.bfloat16
PLANE = 4
PLANES = 4
CHUNKS = ((0, 1), (2, 3))
QUAD = 4
PAIR = 2
MIB = 1024 * 1024
LIGHT = pl.CostEstimate(flops=1, bytes_accessed=1, transcendentals=0)
NT = (((1,), (1,)), ((), ()))
TN = (((0,), (0,)), ((), ()))
NN = (((1,), (0,)), ((), ()))


def entering(value, axis, join, neutral, backward):
    count, mine = (lax.axis_size(axis), lax.axis_index(axis))
    pieces = lax.all_gather(value, axis)
    if backward:
        pieces = pieces[::-1]
        mine = count - 1 - mine
    running = jnp.full_like(value, 0) + jnp.asarray(neutral, value.dtype)

    def lap(position, running):
        longer = join(running, pieces[position])
        return jnp.where(position < mine, longer, running)

    return lax.fori_loop(0, count - 1, lap, running)


def add_states(earlier, later):
    return earlier + later


def local(queries, keys, values, gain, out_weight, cotangent):
    highest = lax.Precision.HIGHEST
    rows = queries.shape[0]
    heads = queries.shape[1] // DH
    q_heads = queries.reshape(rows, heads, DH)
    k_heads = keys.reshape(rows, heads, DH)
    v_heads = values.reshape(rows, heads, DH)
    q_float = q_heads.astype(jnp.float32)
    k_float = k_heads.astype(jnp.float32)
    v_float = v_heads.astype(jnp.float32)
    row_ids = lax.broadcasted_iota(jnp.int32, (rows, rows), 0)
    col_ids = lax.broadcasted_iota(jnp.int32, (rows, rows), 1)
    mask = (row_ids >= col_ids).astype(jnp.float32)
    zero_state = jnp.zeros((heads, DH, DH), jnp.float32)
    own_state = jnp.einsum("thd,the->hde", k_heads, v_heads, preferred_element_type=jnp.float32)
    prefix = entering(own_state, "ctx", add_states, zero_state, False)
    scores = (
        jnp.einsum("thd,shd->hts", q_heads, k_heads, preferred_element_type=jnp.float32)
        * mask[None]
    )
    attn = jnp.einsum("hts,shd->thd", scores, v_float, precision=highest)
    attn = attn + jnp.einsum("thd,hde->the", q_float, prefix, precision=highest)
    gain_heads = gain.reshape(heads, DH)
    rnorm = lax.rsqrt(jnp.mean(attn * attn, axis=-1, keepdims=True) + 1e-06)
    normed = attn * rnorm
    heads_out = (normed * gain_heads[None]).astype(jnp.bfloat16).reshape(rows, heads * DH)
    weight_all = lax.all_gather(out_weight, "ctx", axis=0, tiled=True)
    mixed = jnp.dot(
        lax.all_gather(heads_out, "tp", axis=1, tiled=True),
        weight_all,
        preferred_element_type=jnp.float32,
    ).astype(jnp.bfloat16)
    partial_grads = lax.dot_general(
        cotangent, weight_all, (((1,), (1,)), ((), ())), preferred_element_type=jnp.float32
    )
    grad_heads = lax.psum_scatter(partial_grads, "tp", scatter_dimension=1, tiled=True).reshape(
        rows, heads, DH
    )
    scaled = grad_heads * gain_heads[None]
    grad_attn = rnorm * (scaled - normed * jnp.mean(scaled * normed, axis=-1, keepdims=True))
    own_grad = jnp.einsum("thd,the->hde", q_float, grad_attn, precision=highest)
    later = entering(own_grad, "ctx", add_states, zero_state, True)
    weights = jnp.einsum("the,she->hts", grad_attn, v_float, precision=highest) * mask[None]
    grad_q = jnp.einsum("the,hde->thd", grad_attn, prefix, precision=highest)
    grad_q = grad_q + jnp.einsum("hts,shd->thd", weights, k_float, precision=highest)
    grad_k = jnp.einsum("she,hde->shd", v_float, later, precision=highest)
    grad_k = grad_k + jnp.einsum("hts,thd->shd", weights, q_float, precision=highest)
    grad_v = jnp.einsum("shd,hde->she", k_float, later, precision=highest)
    grad_v = grad_v + jnp.einsum("hts,the->she", scores, grad_attn, precision=highest)
    grad_queries = grad_q.reshape(rows, heads * DH).astype(jnp.bfloat16)
    grad_keys = grad_k.reshape(rows, heads * DH).astype(jnp.bfloat16)
    grad_values = grad_v.reshape(rows, heads * DH).astype(jnp.bfloat16)
    return (mixed, grad_queries, grad_keys, grad_values)


def mm(a, b, dims):
    return lax.dot_general(a, b, dims, preferred_element_type=F32)


def two_terms(value):
    high = value.astype(BF16)
    return high, (value - high.astype(F32)).astype(BF16)


def lower_mask(rows):
    row_ids = lax.broadcasted_iota(jnp.int32, (rows, rows), 0)
    col_ids = lax.broadcasted_iota(jnp.int32, (rows, rows), 1)
    return row_ids >= col_ids


def span(h):
    return slice(h * DH, (h + 1) * DH)


def pieces_kernel(pos, w_ref, *outs):
    width = outs[0].shape[1]
    for n in range(PLANE):
        outs[n][...] = w_ref[:, pl.ds(pl.multiple_of((pos[0] ^ n) * width, DH), width)]


def states_kernel(pos, k_ref, v_ref, *refs):
    for n in range(PLANE):
        for h in range(QUAD):
            cols = pl.ds(pl.multiple_of(((pos[0] ^ n) * QUAD + h) * DH, DH), DH)
            refs[n - PLANE][h] = mm(k_ref[:, cols], v_ref[:, cols], TN)


def prepare(pos, keys, values, out_weight):
    whole = pl.BlockSpec(memory_space=pltpu.VMEM)
    place = pl.BlockSpec(memory_space=pltpu.SMEM)
    piece = (out_weight.shape[0], out_weight.shape[1] // PLANE)
    params = pltpu.CompilerParams(vmem_limit_bytes=56 * MIB)
    pieces = pl.pallas_call(
        pieces_kernel,
        in_specs=[place, whole],
        out_specs=[whole] * PLANE,
        out_shape=[jax.ShapeDtypeStruct(piece, BF16)] * PLANE,
        compiler_params=params,
        cost_estimate=LIGHT,
    )(pos, out_weight)
    states = pl.pallas_call(
        states_kernel,
        in_specs=[place, whole, whole, pl.BlockSpec(memory_space=pl.ANY)],
        out_specs=[whole] * PLANE,
        out_shape=[jax.ShapeDtypeStruct((QUAD, DH, DH), F32)] * PLANE,
        compiler_params=params,
        cost_estimate=LIGHT,
    )(pos, keys, values, pieces[0])
    return states, pieces


def forward_kernel(pos, q_ref, k_ref, v_ref, gain_ref, prefix_ref, heads_ref, attn_ref):
    mask = lower_mask(q_ref.shape[0])
    for h in range(QUAD):
        cols = span(h)
        q = q_ref[:, cols]
        scores = jnp.where(mask, mm(q, k_ref[:, cols], NT), 0.0)
        high, low = two_terms(scores)
        top, rest = two_terms(prefix_ref[h])
        v = v_ref[:, cols]
        attn = mm(high, v, NN) + mm(low, v, NN) + mm(q, top, NN) + mm(q, rest, NN)
        rnorm = lax.rsqrt(jnp.mean(attn * attn, axis=-1, keepdims=True) + 1e-06)
        attn_ref[:, cols] = attn
        heads_ref[:, cols] = (attn * rnorm * gain_ref[:, cols]).astype(BF16)


def norm_kernel(pos, q_ref, gain_ref, attn_ref, mine_ref, one_ref, two_ref, three_ref, *refs):
    g_ref, own_ref = refs[-2:]
    for h in range(PAIR):
        cols = span(h)
        attn = attn_ref[:, cols]
        rnorm = lax.rsqrt(jnp.mean(attn * attn, axis=-1, keepdims=True) + 1e-06)
        normed = attn * rnorm
        grads = mine_ref[:, cols]
        for ref in (one_ref, two_ref, three_ref):
            grads = grads + ref[:, cols].astype(F32)
        scaled = grads * gain_ref[:, cols]
        shared = jnp.mean(scaled * normed, axis=-1, keepdims=True)
        g = rnorm * (scaled - normed * shared)
        g_ref[:, cols] = g
        high, low = two_terms(g)
        q = q_ref[:, cols]
        own_ref[h] = mm(q, high, TN) + mm(q, low, TN)


def inner_kernel(pos, q_ref, k_ref, v_ref, g_ref, first_ref, second_ref, *refs):
    gq_ref, gk_ref, gv_ref = refs[-3:]
    mask = lower_mask(q_ref.shape[0])
    for h in range(PAIR):
        cols = span(h)
        q, k, v = q_ref[:, cols], k_ref[:, cols], v_ref[:, cols]
        high, low = two_terms(g_ref[:, cols])
        top, rest = two_terms((first_ref, second_ref)[h][0])
        weights = jnp.where(mask, mm(high, v, NT) + mm(low, v, NT), 0.0).astype(BF16)
        scores = jnp.where(mask, mm(q, k, NT), 0.0).astype(BF16)
        across = mm(high, top, NT) + mm(high, rest, NT) + mm(low, top, NT)
        gq_ref[:, cols] = (across + mm(weights, k, NN)).astype(BF16)
        gk_ref[:, cols] = mm(weights, q, TN)
        gv_ref[:, cols] = mm(scores, high, TN)


def outer_kernel(pos, k_ref, v_ref, gk_ref, gv_ref, later_ref, *refs):
    gk_out, gv_out = refs[-2:]
    for h in range(PAIR):
        cols = span(h)
        top, rest = two_terms(later_ref[h])
        v, k = v_ref[:, cols], k_ref[:, cols]
        gk_out[:, cols] = (gk_ref[:, cols] + mm(v, top, NT) + mm(v, rest, NT)).astype(BF16)
        gv_out[:, cols] = (gv_ref[:, cols] + mm(k, top, NN) + mm(k, rest, NN)).astype(BF16)


def by_heads(kernel, pos, ins, outs, flops, chunk=None, onto=(), after=()):
    rows = ins[0][0].shape[0]
    count = QUAD if chunk is None else PAIR
    width = count * DH
    each = PLANE if chunk is None else len(chunk)
    steps = PLANE if chunk is None else 2 * each

    def pair_of(s):
        return s if chunk is None else (s // each) * PLANE + chunk[0] + s % each

    def held(head, share, pos):
        return (((head // share) ^ pos[0]) * share + head % share, 0, 0)

    one = (1, DH, DH)
    specs = {
        "cols": pl.BlockSpec((rows, width), lambda s, pos: (0, pair_of(s))),
        "row": pl.BlockSpec((1, width), lambda s, pos: (0, pair_of(s))),
        "chunk": pl.BlockSpec((rows, width), lambda s, pos: (0, s)),
        "own": pl.BlockSpec((count, DH, DH), lambda s, pos: (s, 0, 0)),
        "xor": pl.BlockSpec((count, DH, DH), lambda s, pos: (s ^ pos[0], 0, 0)),
        "prefix0": pl.BlockSpec(one, lambda s, pos: held(pair_of(s) * PAIR, QUAD, pos)),
        "prefix1": pl.BlockSpec(one, lambda s, pos: held(pair_of(s) * PAIR + 1, QUAD, pos)),
        "later": pl.BlockSpec(
            (PAIR, DH, DH), lambda s, pos: ((((s // 4) * 2 + s % 2) ^ pos[0]) * len(CHUNKS) + s % 4 // 2, 0, 0)
        ),
    }
    moved = sum(math.prod(shape) * jnp.dtype(dtype).itemsize for shape, dtype, _ in outs)
    moved += sum(a.size * a.dtype.itemsize for a, _ in ins)
    aliases = {1 + len(ins) + n: at for n, (_, at) in enumerate(onto)}
    unread = [a for a, _ in onto] + list(after)
    return pl.pallas_call(
        kernel,
        grid_spec=pltpu.PrefetchScalarGridSpec(
            num_scalar_prefetch=1,
            grid=(steps,),
            in_specs=[specs[kind] for _, kind in ins] + [pl.BlockSpec(memory_space=pl.ANY)] * len(unread),
            out_specs=[specs[kind] for _, _, kind in outs],
        ),
        out_shape=[jax.ShapeDtypeStruct(shape, dtype) for shape, dtype, _ in outs],
        input_output_aliases=aliases,
        compiler_params=pltpu.CompilerParams(vmem_limit_bytes=56 * MIB),
        cost_estimate=LIGHT,
    )(pos, *[a for a, _ in ins], *unread)


def others_kernel(pos, cot_ref, w_ref, *refs):
    out_ref = refs[-1]
    for t in range(PLANE):
        out_ref[t] = mm(cot_ref[t], w_ref[0], NT).astype(BF16)


def mine_kernel(pos, cot_ref, w_ref, other_ref, *refs):
    own_ref, sent = refs[-4], refs[-3:]
    for t in range(PLANE):
        total = mm(cot_ref[t], w_ref[0], NT) + other_ref[t].astype(F32)
        if t == 0:
            own_ref[...] = total
        else:
            sent[t - 1][...] = total.astype(BF16)


def partial_grads(pos, cot, weights, taken=None, after=()):
    planes, rows, width = weights.shape
    blocks, tokens, _ = cot.shape
    each = planes // 2
    whole = (blocks, tokens, each * rows)
    block = pl.BlockSpec((blocks, tokens, rows), lambda i, pos: (0, 0, i))
    flat = pl.BlockSpec((tokens, rows), lambda i, pos: (0, i))

    def plane_of(i, pos):
        return ((1 - pos[2] if taken is None else pos[2]) * each + i, 0, 0)

    in_specs = [pl.BlockSpec(cot.shape, lambda i, pos: (0, 0, 0)), pl.BlockSpec((1, rows, width), plane_of)]
    if taken is None:
        kernel, out_specs, out_shape, given = others_kernel, block, jax.ShapeDtypeStruct(whole, BF16), ()
    else:
        kernel, given = mine_kernel, (taken,)
        in_specs.append(block)
        out_specs = [flat] * blocks
        out_shape = [jax.ShapeDtypeStruct(whole[1:], F32)] + [jax.ShapeDtypeStruct(whole[1:], BF16)] * (blocks - 1)
    in_specs += [pl.BlockSpec(memory_space=pl.ANY)] * len(after)
    return pl.pallas_call(
        kernel,
        grid_spec=pltpu.PrefetchScalarGridSpec(
            num_scalar_prefetch=1, grid=(each,), in_specs=in_specs, out_specs=out_specs
        ),
        out_shape=out_shape,
        compiler_params=pltpu.CompilerParams(vmem_limit_bytes=56 * MIB),
        cost_estimate=LIGHT,
    )(pos, cot, weights, *given, *after)


def place_kernel(pos, *refs):
    pieces, outs = refs[:PLANE], refs[-len(CHUNKS) :]
    rows = pieces[0].shape[0]
    for k, piece in enumerate(pieces):
        j = pos[0] ^ k
        for chunk, out in zip(CHUNKS, outs, strict=True):

            def store(chunk=chunk, out=out, piece=piece, j=j):
                within = jnp.clip(j - chunk[0], 0, len(chunk) - 1)
                out[pl.ds(pl.multiple_of(within * rows, rows), rows)] = piece[...]

            pl.when((j >= chunk[0]) & (j <= chunk[-1]))(store)


def place_chunks(pos, pieces, after):
    rows, width = pieces[0].shape
    whole = pl.BlockSpec(memory_space=pltpu.VMEM)
    return pl.pallas_call(
        place_kernel,
        in_specs=[pl.BlockSpec(memory_space=pltpu.SMEM)] + [whole] * len(pieces)
        + [pl.BlockSpec(memory_space=pl.ANY)] * len(after),
        out_specs=[whole] * len(CHUNKS),
        out_shape=[jax.ShapeDtypeStruct((len(chunk) * rows, width), BF16) for chunk in CHUNKS],
        compiler_params=pltpu.CompilerParams(vmem_limit_bytes=56 * MIB),
        cost_estimate=LIGHT,
    )(pos, *pieces, *after)


def mixed_kernel(pos, *refs):
    groups, weights = (refs[0:5], refs[5:10]), refs[10 : 10 + len(CHUNKS)]
    outs, (held, stacked, x_sems, w_sems) = refs[-8:-4], refs[-4:]
    tokens, width = refs[0].shape
    planes, depth = weights[0].shape[0], sum(ref.shape[1] for ref in weights)
    loads = []
    for i in range(planes):
        start = i * depth
        for ref in weights:
            target = stacked.at[pl.ds(start, ref.shape[1])]
            loads.append(pltpu.make_async_copy(ref.at[i], target, w_sems.at[len(loads)]))
            start += ref.shape[1]
    blocks = [[] for _ in range(PLANE)]
    count = 0
    for group, core in zip(groups, (pos[2], 1 - pos[2]), strict=True):
        columns = pl.ds(pl.multiple_of(core * width, width), width)
        for n, ref in enumerate(group):
            target = held.at[min(n, PLANE - 1), :, columns]
            if n >= PLANE - 1:
                part = tokens // 2
                target = held.at[PLANE - 1, pl.ds((n - PLANE + 1) * part, part), columns]
            blocks[min(n, PLANE - 1)].append(pltpu.make_async_copy(ref, target, x_sems.at[count]))
            count += 1
    for copy in blocks[0] + loads + blocks[1] + blocks[2] + blocks[3]:
        copy.start()
    for copy in loads:
        copy.wait()
    for t in range(PLANE):
        for copy in blocks[t]:
            copy.wait()
        outs[t][...] = mm(held[t], stacked[...], NN).astype(BF16)


def mixed_blocks(pos, x_own, x_other, weights, after):
    tokens, depth = x_own[0].shape
    width = weights[0].shape[2]
    given = [*x_own, *x_other, *weights, *after]
    return pl.pallas_call(
        mixed_kernel,
        in_specs=[pl.BlockSpec(memory_space=pltpu.SMEM)] + [pl.BlockSpec(memory_space=pl.ANY)] * len(given),
        out_specs=[pl.BlockSpec(memory_space=pltpu.VMEM)] * PLANE,
        out_shape=[jax.ShapeDtypeStruct((tokens, width), BF16)] * PLANE,
        scratch_shapes=[
            pltpu.VMEM((PLANE, tokens, 2 * depth), BF16),
            pltpu.VMEM((2 * depth, width), BF16),
            pltpu.SemaphoreType.DMA((2 * len(x_own),)),
            pltpu.SemaphoreType.DMA((PLANES * len(weights),)),
        ],
        compiler_params=pltpu.CompilerParams(vmem_limit_bytes=56 * MIB),
        cost_estimate=LIGHT,
    )(pos, *given)


def plane_swap(value, k):
    return lax.ppermute(value, "ctx", [(i, i ^ k) for i in range(PLANE * PLANES)])


def core_swap(value):
    return lax.ppermute(value, "tp", [(0, 1), (1, 0)])


def z_shift(value, by):
    count = PLANE * PLANES
    pairs = [(i, i + by * PLANE) for i in range(count) if 0 <= i + by * PLANE < count]
    return lax.ppermute(value, "ctx", pairs)


def z_gather(value):
    lines = [[z * PLANE + j for z in range(PLANES)] for j in range(PLANE)]
    return lax.all_gather(value, "ctx", axis_index_groups=lines)


def add_kernel(count, *refs):
    total = refs[0][...]
    for ref in refs[1:count]:
        total = total + ref[...]
    refs[-1][...] = total


def add_after(values, after):
    whole = pl.BlockSpec(memory_space=pltpu.VMEM)
    return pl.pallas_call(
        functools.partial(add_kernel, len(values)),
        in_specs=[whole] * len(values) + [pl.BlockSpec(memory_space=pl.ANY)] * len(after),
        out_specs=whole,
        out_shape=jax.ShapeDtypeStruct(values[0].shape, F32),
        compiler_params=pltpu.CompilerParams(vmem_limit_bytes=56 * MIB),
        cost_estimate=LIGHT,
    )(*values, *after)


def plane_swaps(parts):
    return [parts[0]] + [plane_swap(parts[k], k) for k in range(1, PLANE)]


def parts_kernel(pos, *refs):
    owns, outs = refs[: len(CHUNKS)], refs[-PLANE:]
    for k in range(PLANE):
        start = 0
        for own in owns:
            count = own.shape[0] // PLANE
            outs[k][start : start + count] = own[pl.ds((pos[0] ^ k) * count, count)]
            start += count


def plane_parts(owns, pos, after):
    whole = pl.BlockSpec(memory_space=pltpu.VMEM)
    part = (sum(own.shape[0] for own in owns) // PLANE, *owns[0].shape[1:])
    parts = pl.pallas_call(
        parts_kernel,
        in_specs=[pl.BlockSpec(memory_space=pltpu.SMEM)] + [whole] * len(owns),
        out_specs=[whole] * PLANE,
        out_shape=[jax.ShapeDtypeStruct(part, owns[0].dtype)] * PLANE,
        compiler_params=pltpu.CompilerParams(vmem_limit_bytes=56 * MIB),
        cost_estimate=LIGHT,
    )(pos, *owns)
    parts = plane_swaps(parts)
    return parts, add_after(parts, after)


def plane_sums(total, backward, after=()):
    sign = -1 if backward else 1
    near = z_shift(total, sign)
    return near, z_shift(add_after([total, near], after), 2 * sign)


def returns_kernel(backward, pos, near_ref, far_ref, *refs):
    parts, outs = refs[:PLANE], refs[PLANE:]
    entering = near_ref[...] + far_ref[...]
    for t in range(PLANE):
        value = entering
        for k in range(PLANE):
            if k != t:
                here, there = pos[0] ^ k, pos[0] ^ t
                ahead = here > there if backward else here < there
                value = value + jnp.where(ahead, parts[k][...], 0.0)
        outs[t][...] = value


def plane_returns(pos, parts, sums, backward):
    whole = pl.BlockSpec(memory_space=pltpu.VMEM)
    given = pl.pallas_call(
        functools.partial(returns_kernel, backward),
        in_specs=[pl.BlockSpec(memory_space=pltpu.SMEM)] + [whole] * (2 + PLANE),
        out_specs=[whole] * PLANE,
        out_shape=[jax.ShapeDtypeStruct(parts[0].shape, F32)] * PLANE,
        compiler_params=pltpu.CompilerParams(vmem_limit_bytes=56 * MIB),
        cost_estimate=LIGHT,
    )(pos, *sums, *parts)
    return jnp.concatenate(plane_swaps(given), axis=0)


def plane_local(queries, keys, values, gain, out_weight, cotangent):
    rows, columns = queries.shape
    at = lax.axis_index("ctx")
    p, z = at % PLANE, at // PLANE
    pos = jnp.stack([p, z, lax.axis_index("tp")]).astype(jnp.int32)
    wide = out_weight.shape[1] // PLANE

    states, pieces = prepare(pos, keys, values, out_weight)
    parts = plane_swaps(states)
    total = add_after(parts, ())
    weights = [z_gather(chunk) for chunk in place_chunks(pos, plane_swaps(pieces), (states[0],))]
    cot_pieces = plane_swaps([lax.dynamic_slice_in_dim(cotangent, (p ^ k) * wide, wide, 1) for k in range(PLANE)])
    prefix = plane_returns(pos, parts, plane_sums(total, False, cot_pieces[1:]), False)
    cot = jnp.stack(cot_pieces)
    gain_row = gain.reshape(1, columns)
    heads_out, attn = by_heads(
        forward_kernel,
        pos,
        [(queries, "cols"), (keys, "cols"), (values, "cols"), (gain_row, "row"), (prefix, "xor")],
        [((rows, columns), BF16, "cols"), ((rows, columns), F32, "cols")],
        2 * rows * columns * (3 * rows + 2 * DH),
    )
    x_one, x_two = plane_swap(heads_out, 1), plane_swap(heads_out, 2)
    x_three = plane_swap(x_one[: rows // 2], 2), plane_swap(x_two[rows // 2 :], 1)
    x_own = [heads_out, x_one, x_two, *x_three]
    x_other = [core_swap(x) for x in x_own]

    before_others, before_norm = (heads_out,), ()
    before_mine = (x_one, x_two)
    owns, inners = [], []
    for n, (chunk, weight) in enumerate(zip(CHUNKS, weights, strict=True)):
        last = n == len(CHUNKS) - 1
        count = 2 * PAIR * len(chunk)
        if n == 0:
            other = core_swap(partial_grads(pos, cot, weight, after=before_others))
            mine, *sent = partial_grads(pos, cot, weight, other, before_mine)
        else:
            mine, *sent = partial_grads(pos, cot, weight, core_swap(theirs), before_mine)
        if last:
            blocks = mixed_blocks(pos, x_own, x_other, weights, (sent[0],))
            before_norm = (blocks[0], inners[0])
        taken = plane_swaps([None, *sent])[1:]
        if not last:
            theirs = partial_grads(pos, cot, weights[n + 1], after=(*taken, *x_three))
            before_norm = (theirs,)
        g, own_grad = by_heads(
            norm_kernel,
            pos,
            [(queries, "cols"), (gain_row, "row"), (attn, "cols"), (mine, "chunk")]
            + [(value, "chunk") for value in taken],
            [((rows, count * DH), F32, "chunk"), ((count, DH, DH), F32, "own")],
            0,
            chunk,
            after=before_norm,
        )
        before_mine = (own_grad,)
        owns.append(own_grad)
        inners = by_heads(
            inner_kernel,
            pos,
            [(queries, "cols"), (keys, "cols"), (values, "cols"), (g, "chunk"), (prefix, "prefix0"), (prefix, "prefix1")],
            [((rows, columns), BF16, "cols"), ((rows, columns), F32, "cols"), ((rows, columns), F32, "cols")],
            0,
            chunk,
            list(zip(inners, range(3), strict=False)),
        )
    grad_q, inner_k, inner_v = inners
    parts, total = plane_parts(owns, pos, ())
    later = plane_returns(pos, parts, plane_sums(total, True, (grad_q,)), True)
    grad_k, grad_v = by_heads(
        outer_kernel,
        pos,
        [(keys, "cols"), (values, "cols"), (inner_k, "cols"), (inner_v, "cols"), (later, "later")],
        [((rows, columns), BF16, "cols"), ((rows, columns), BF16, "cols")],
        0,
        (0, 1, 2, 3),
    )
    mixed = jnp.zeros((rows, PLANE * wide), BF16)
    for k in range(PLANE):
        block = blocks[0] if k == 0 else plane_swap(blocks[k], k)
        mixed = lax.dynamic_update_slice_in_dim(mixed, block, (p ^ k) * wide, 1)
    return mixed, grad_q, grad_k, grad_v


def planes_fit(mesh):
    return mesh.shape["ctx"] == PLANE * PLANES and mesh.shape["tp"] == 2


def solution(mesh):
    placed = (
        P("ctx", "tp"),
        P("ctx", "tp"),
        P("ctx", "tp"),
        P("tp"),
        P("ctx", "tp"),
        P("ctx", "tp"),
    )
    return jax.shard_map(
        plane_local if planes_fit(mesh) else local,
        mesh=mesh,
        in_specs=placed,
        out_specs=(P("ctx", "tp"), P("ctx", "tp"), P("ctx", "tp"), P("ctx", "tp")),
        check_vma=False,
    )
```
